512 devices in a mesh: gx: 4 (over z_lo), gy: 4 (over z_hi), gz: 32 (over x, y, core).
Axes of the slice: x: 4, y: 4, z: 16 (z_hi: 4, z_lo: 4; z = z_hi * 4 + z_lo), core: 2. Of those that a mesh axis runs over, the one named last changes fastest.
Arguments:
- heat_level: float32 [32, 64, 4096], P('gx', 'gy', 'gz'), may hold values from 0 to 1
- flow_rate: float32 [3, 32, 64, 4096], P(None, 'gx', 'gy', 'gz'), may hold values from -9 to 9
- flow_guess: float32 [4, 32, 64, 4096], P(None, 'gx', 'gy', 'gz'), may hold values from -6 to 6
- rock_label: int32 [32, 64, 4096], P('gx', 'gy', 'gz'), may hold values from 0 to 3
- clamp_mask: int32 [32, 64, 4096], P('gx', 'gy', 'gz'), may hold values from 0 to 15
- rheology_coefficient: float32 [4], replicated, may hold values from 0.3 to 3
- local_operator_tiles: float32 [3, 32, 32], replicated, may hold values from -1 to 1
Outputs:
- heat_level_later: float32 [32, 64, 4096], P('gx', 'gy', 'gz')
- equation_misfit: float32 [4, 32, 64, 4096], P(None, 'gx', 'gy', 'gz')
The draws below stay inside these ranges and needn't reach their ends.
All inputs are finite; a program needn't handle non-finite values. Where the reference program divides by a largest or mean magnitude, that divisor is 1e-20 or more.
Results may differ from the reference program's by a relative error of at most 0.0003.
Values sent between devices are 32-bit elements; how exact they have to be, the bound alone decides.
A program may use at most 64 MiB of HBM per device.

```python
import math
import jax
import jax.numpy as jnp
from jax import lax

CZ = 128
MATERIALS = 4
LATERAL_POINTS_X = 32
LATERAL_POINTS_Y = 64
VERTICAL_POINTS = 4096


def draw_flow_rate(key, part):
    key = jax.random.fold_in(key, 11)
    key_base, key_block, key_comp, key_place, key_peak = jax.random.split(key, 5)
    full_shape = (3, LATERAL_POINTS_X, LATERAL_POINTS_Y, VERTICAL_POINTS)
    base = jnp.clip(jax.random.normal(key_base, full_shape, jnp.float32), -3.0, 3.0)
    block_count = VERTICAL_POINTS // CZ
    block_factor = jnp.exp(jax.random.uniform(key_block, (block_count,), jnp.float32, jnp.log(0.3), 0.0))
    depth_factor = jnp.repeat(block_factor, CZ)
    comp_factor = jax.random.uniform(key_comp, (3,), jnp.float32, 0.5, 1.0)
    field = base * comp_factor.reshape(3, 1, 1, 1) * depth_factor.reshape(1, 1, 1, VERTICAL_POINTS)
    upper = jnp.array([3, LATERAL_POINTS_X, LATERAL_POINTS_Y, VERTICAL_POINTS, 2], jnp.int32)
    picks = jax.random.randint(key_place, (5,), jnp.zeros((5,), jnp.int32), upper)
    amplitude = jax.random.uniform(key_peak, (), jnp.float32, 3.5, 9.0)
    sign_value = 2.0 * picks[4].astype(jnp.float32) - 1.0
    comp_index = jnp.arange(3, dtype=jnp.int32).reshape(3, 1, 1, 1)
    x_index = jnp.arange(LATERAL_POINTS_X, dtype=jnp.int32).reshape(1, LATERAL_POINTS_X, 1, 1)
    y_index = jnp.arange(LATERAL_POINTS_Y, dtype=jnp.int32).reshape(1, 1, LATERAL_POINTS_Y, 1)
    z_index = jnp.arange(VERTICAL_POINTS, dtype=jnp.int32).reshape(1, 1, 1, VERTICAL_POINTS)
    marked = (comp_index == picks[0]) & (x_index == picks[1]) & (y_index == picks[2]) & (z_index == picks[3])
    return jnp.where(marked, sign_value * amplitude, field)


def plant(values, rng, smallest, largest):
    shape = values.shape
    index_at = [jax.random.randint(jax.random.fold_in(rng, axis), (), 0, shape[axis]) for axis in range(len(shape))]
    values = values.at[tuple(index_at)].set(smallest)
    longest = shape.index(max(shape))
    index_at[longest] = (index_at[longest] + 1) % shape[longest]
    return values.at[tuple(index_at)].set(largest)


def levels(stream_key, extent, pieces, least, largest):
    factor_of = 1.0
    for position, shards_of in pieces:
        heights = jax.random.uniform(jax.random.fold_in(jax.random.fold_in(stream_key, 6), position), (shards_of,), jnp.float32, least / len(pieces), largest / len(pieces))
        factor_of = factor_of * jnp.repeat(jnp.exp(heights), extent[position] // shards_of).reshape((-1,) + (1,) * (len(extent) - 1 - position))
    return factor_of


def centred(own_key, shape, width, bound, shards=(), kind=jnp.bfloat16):
    gain = levels(own_key, shape, shards, -0.22, 0.18) if shards else 1.0
    result = jax.random.normal(own_key, shape, jnp.float32) * width * gain
    return jnp.minimum(jnp.maximum(result, -bound), bound).astype(kind)


def setup_inputs(seed: int = 0) -> dict:
    seeds = jax.random.split(jax.random.key(seed), 8)
    heat_level = jnp.clip(1.0 * jax.random.uniform(seeds[0], (LATERAL_POINTS_X, LATERAL_POINTS_Y, VERTICAL_POINTS), jnp.float32) ** levels(seeds[0], (LATERAL_POINTS_X, LATERAL_POINTS_Y, VERTICAL_POINTS), ((0, 4), (1, 4), (2, 32)), -0.2, 0.2), 0.0, 1.0)
    flow_rate = draw_flow_rate(jax.random.fold_in(seeds[7], 71), 0)
    flow_guess = centred(seeds[2], (4, LATERAL_POINTS_X, LATERAL_POINTS_Y, VERTICAL_POINTS), 1.0, 6.0, ((1, 4), (2, 4), (3, 32)), jnp.float32)
    rock_label = plant(jax.random.randint(seeds[3], (LATERAL_POINTS_X, LATERAL_POINTS_Y, VERTICAL_POINTS), 0, MATERIALS), jax.random.fold_in(seeds[3], 1), 0, MATERIALS - 1).astype(jnp.int32)
    clamp_mask = plant(jax.random.randint(seeds[4], (LATERAL_POINTS_X, LATERAL_POINTS_Y, VERTICAL_POINTS), 0, 16), jax.random.fold_in(seeds[4], 1), 0, 15).astype(jnp.int32)
    rheology_coefficient = jnp.clip(jnp.exp(jax.random.uniform(seeds[5], (MATERIALS,), jnp.float32, math.log(0.3), math.log(3.0))), 0.3, 3.0)
    local_operator_tiles = centred(seeds[6], (3, 32, 32), 32 ** -0.5, 1.0, (), jnp.float32)
    return dict(heat_level=heat_level, flow_rate=flow_rate, flow_guess=flow_guess, rock_label=rock_label, clamp_mask=clamp_mask, rheology_coefficient=rheology_coefficient, local_operator_tiles=local_operator_tiles)


COURANT = 0.5
DIFFUSIVITY = 1.0
ACTIVATION = 3.0
STABILIZER = 0.25
THERMAL_LIFT = 2.0
CORNERS = tuple((a, b, c) for a in (0, 1) for b in (0, 1) for c in (0, 1))


def lookup(rock_label, rheology_coefficient):
    total = jnp.zeros(rock_label.shape, jnp.float32)
    for selector in range(rheology_coefficient.shape[0]):
        total = total + jnp.where(rock_label == selector, rheology_coefficient[selector], 0.0)
    return total


def advance_heat(bordered_copy, flow_rate, duration_delta):
    centre = bordered_copy[1:-1, 1:-1, 1:-1]
    plus_x = bordered_copy[2:, 1:-1, 1:-1]
    minus_x = bordered_copy[:-2, 1:-1, 1:-1]
    plus_y = bordered_copy[1:-1, 2:, 1:-1]
    minus_y = bordered_copy[1:-1, :-2, 1:-1]
    plus_z = bordered_copy[1:-1, 1:-1, 2:]
    minus_z = bordered_copy[1:-1, 1:-1, :-2]
    laplace = plus_x + minus_x + plus_y + minus_y + plus_z + minus_z - 6.0 * centre
    transport = flow_rate[0] * (plus_x - minus_x) + flow_rate[1] * (plus_y - minus_y) + flow_rate[2] * (plus_z - minus_z)
    return centre + duration_delta * (DIFFUSIVITY * laplace - 0.5 * transport)


def reference(heat_level, flow_rate, flow_guess, rock_label, clamp_mask, rheology_coefficient, local_operator_tiles):
    top_speed = jnp.max(jnp.abs(flow_rate))
    duration_delta = COURANT / (top_speed + 6.0 * DIFFUSIVITY)
    heat_level_later = advance_heat(jnp.pad(heat_level, 1), flow_rate, duration_delta)
    local_coefficient = lookup(rock_label, rheology_coefficient)

    def slab_step(carry, selector):
        heat_couple = lax.dynamic_slice_in_dim(heat_level_later, selector, 2, 0)
        trial_pair = lax.dynamic_slice_in_dim(flow_guess, selector, 2, 1)
        prefac = lax.dynamic_index_in_dim(local_coefficient, selector, 0, keepdims=False)[:LATERAL_POINTS_Y - 1, :VERTICAL_POINTS - 1]
        tcell = sum(heat_couple[a, b:b + LATERAL_POINTS_Y - 1, c:c + VERTICAL_POINTS - 1] for (a, b, c) in CORNERS) / 8.0
        viscosity = prefac * jnp.exp(ACTIVATION * (0.5 - tcell))
        stabilize = STABILIZER / viscosity
        element_values = jnp.stack([trial_pair[k, a, b:b + LATERAL_POINTS_Y - 1, c:c + VERTICAL_POINTS - 1] for k in range(4) for (a, b, c) in CORNERS])
        forces = viscosity * jnp.einsum("ab,byz->ayz", local_operator_tiles[0], element_values, precision=lax.Precision.HIGHEST)
        forces = forces + stabilize * jnp.einsum("ab,byz->ayz", local_operator_tiles[1], element_values, precision=lax.Precision.HIGHEST)
        forces = forces + jnp.einsum("ab,byz->ayz", local_operator_tiles[2], element_values, precision=lax.Precision.HIGHEST)

        def spread(side):
            planes = []
            for k in range(4):
                summed = jnp.zeros((LATERAL_POINTS_Y, VERTICAL_POINTS), jnp.float32)
                for q, (a, b, c) in enumerate(CORNERS):
                    if a == side:
                        summed = summed + jnp.pad(forces[k * 8 + q], ((b, 1 - b), (c, 1 - c)))
                planes.append(summed)
            return jnp.stack(planes)

        return spread(1), spread(0) + carry

    final_plane, planes = lax.scan(slab_step, jnp.zeros((4, LATERAL_POINTS_Y, VERTICAL_POINTS), jnp.float32), jnp.arange(LATERAL_POINTS_X - 1, dtype=jnp.int32))
    stiffness = jnp.concatenate([planes, final_plane[None]], 0).transpose(1, 0, 2, 3)
    unknown_position = jnp.arange(4, dtype=jnp.int32).reshape(4, 1, 1, 1)
    source_term = THERMAL_LIFT * heat_level_later[None] * (unknown_position == 2)
    fixed_dof = (clamp_mask[None] // (2 ** unknown_position)) % 2 == 1
    equation_misfit = jnp.where(fixed_dof, flow_guess, stiffness - source_term)
    return heat_level_later, equation_misfit
```

```python
import functools

import jax
import jax.numpy as jnp
from jax import lax
from jax.experimental import pallas as pl
from jax.experimental.pallas import tpu as pltpu
from jax.sharding import PartitionSpec as P

MESH = pl.DeviceIdType.MESH
F32 = jnp.float32
BF16 = jnp.bfloat16

LX, LY, LZ = 8, 16, 128
NODES = LX * LY
EX, EY = LX + 2, LY + 2
CX, CY = LX + 1, LY + 1
TR = 32
PW = 256
COEF, TEMP, RATE = 4, 5, 6


def lanes(shape):
    return lax.broadcasted_iota(jnp.int32, shape, 1)


def exchange(
    sizes,
    rheo_in,
    ops_in,
    heat,
    rate,
    guess,
    rock,
    mask,
    nat,
    mk,
    f,
    f2,
    fp,
    sums,
    ce,
    ends,
    speed,
    rheo,
    ops,
    vel,
    rk,
    te,
    ge,
    sx,
    rx,
    sy,
    ry,
    se,
    re,
    stz,
    rtz,
    sp,
    rp,
    tops,
    xb,
    wts,
    lsem,
    ss,
    rs,
    ms,
    mr,
):
    nx, ny, nz = sizes
    gx, gy, gz = lax.axis_index("gx"), lax.axis_index("gy"), lax.axis_index("gz")
    has_x = (gx > 0, gx < nx - 1)
    has_y = (gy > 0, gy < ny - 1)
    has_z = (gz > 0, gz < nz - 1)

    barrier = pltpu.get_barrier_semaphore()

    stages = (
        (nx * ny, gy * nx + gx, lambda t: {"gx": lax.rem(t, nx), "gy": t // nx}),
        (nz, gz, lambda t: {"gz": t}),
    )
    step_x = ({"gx": gx - 1}, {"gx": gx + 1})
    step_y = ({"gy": gy - 1}, {"gy": gy + 1})
    step_z = ({"gz": gz - 1}, {"gz": gz + 1})
    step_e = [dict(**step_x[e // 2], **step_y[e % 2]) for e in range(4)]
    has_e = [jnp.logical_and(has_x[e // 2], has_y[e % 2]) for e in range(4)]

    def greet(device):
        pl.semaphore_signal(barrier, inc=1, device_id=device, device_id_type=MESH)

    def far_first(j, size):
        return 1 + lax.rem(j - 1 + size // 2, max(size - 1, 1))

    for size, own, at in stages:

        def greet_one(j, carry):
            greet(at(lax.rem(own + far_first(j, size), size)))
            return carry

        lax.fori_loop(1, size, greet_one, 0)

    locals_ = [
        pltpu.make_async_copy(rate, vel, lsem.at[0]),
        pltpu.make_async_copy(heat, nat.at[pl.ds(TEMP * NODES, NODES)], lsem.at[1]),
        pltpu.make_async_copy(guess, nat.at[pl.ds(0, 4 * NODES)], lsem.at[2]),
        pltpu.make_async_copy(rock, rk, lsem.at[3]),
        pltpu.make_async_copy(rheo_in, rheo, lsem.at[4]),
        pltpu.make_async_copy(ops_in, ops, lsem.at[5]),
        pltpu.make_async_copy(mask, mk, lsem.at[6]),
    ]
    for copy in locals_:
        copy.start()

    for d in range(2):

        @pl.when(jnp.logical_not(has_x[d]))
        def _():
            rx[d] = jnp.zeros((8 * LY, LZ), F32)
            rx[d, pl.ds(COEF * LY, LY), :] = jnp.ones((LY, LZ), F32)

        @pl.when(jnp.logical_not(has_y[d]))
        def _():
            ry[d] = jnp.zeros((8 * LX, LZ), F32)
            ry[d, pl.ds(COEF * LX, LX), :] = jnp.ones((LX, LZ), F32)

        @pl.when(jnp.logical_not(has_z[d]))
        def _():
            rtz[d] = jnp.zeros((8, LZ), F32)
            rp[d] = jnp.where(
                lax.broadcasted_iota(jnp.int32, (8, PW), 0) == COEF, 1.0, 0.0
            ).astype(F32)

    for e in range(4):

        @pl.when(jnp.logical_not(has_e[e]))
        def _():
            re[e] = jnp.where(
                lax.broadcasted_iota(jnp.int32, (8, LZ), 0) == COEF, 1.0, 0.0
            ).astype(F32)

    nat[pl.ds(7 * NODES, NODES), :] = jnp.zeros((NODES, LZ), F32)

    locals_[0].wait()
    top = jnp.abs(vel[pl.ds(0, 8), :])

    def top_step(i, top):
        for k in range(8):
            top = jnp.maximum(top, jnp.abs(vel[pl.ds(pl.multiple_of(i * 64 + k * 8, 8), 8), :]))
        return top

    top = lax.fori_loop(0, 3 * NODES // 64, top_step, top)
    tops[0, stages[0][1]] = jnp.max(top, axis=0, keepdims=True)

    locals_[1].wait()
    lane = lanes((8, LZ))
    t0 = TEMP * NODES
    for d in range(2):
        xs, ys = (0, LX - 1)[d], (0, LY - 1)[d]
        sx[d, pl.ds(TEMP * LY, LY), :] = nat[pl.ds(t0 + xs * LY, LY), :]
        sy[d, pl.ds(TEMP * LX, LX), :] = nat[pl.ds(t0 + ys, LX, stride=LY), :]
    low = jnp.zeros((8, LZ), F32)
    high = jnp.zeros((8, LZ), F32)
    for j in range(NODES // 8):
        r = nat[pl.ds(t0 + j * 8, 8), :]
        if j:
            r = pltpu.roll(r, j, 1)
        low = jnp.where(lane == j, r, low)
        high = jnp.where(lane == (j - 1) % LZ, r, high)
    stz[0] = low
    stz[1] = high

    locals_[2].wait()
    locals_[3].wait()
    locals_[4].wait()

    for i in range(NODES // 8):
        label = rk[pl.ds(i * 8, 8), :]
        total = jnp.zeros((8, LZ), F32)
        for k in range(4):
            total = total + jnp.where(label == k, rheo[k], 0.0)
        nat[pl.ds(COEF * NODES + i * 8, 8), :] = total
    for d in range(2):
        xs, ys = (0, LX - 1)[d], (0, LY - 1)[d]
        for k in range(5):
            sx[d, pl.ds(k * LY, LY), :] = nat[pl.ds(k * NODES + xs * LY, LY), :]
            sy[d, pl.ds(k * LX, LX), :] = nat[pl.ds(k * NODES + ys, LX, stride=LY), :]
    row = lax.broadcasted_iota(jnp.int32, (32, 32), 0)
    col = lax.broadcasted_iota(jnp.int32, (32, 32), 1)
    from_row = 8 * (row & 3) + 2 * (row >> 3) + ((row >> 2) & 1)
    pick_row = jnp.where(col == from_row, 1.0, 0.0).astype(BF16)
    row = lax.broadcasted_iota(jnp.int32, (32, 128), 0)
    col = lax.broadcasted_iota(jnp.int32, (32, 128), 1)
    from_col = 8 * (col & 3) + 2 * ((col >> 4) & 3) + ((col >> 2) & 1)
    pick_col = jnp.where(row == from_col, 1.0, 0.0).astype(BF16)
    locals_[5].wait()
    for m in range(3):
        block = ops[m]
        head = block.astype(BF16)
        tail = (block - head.astype(F32)).astype(BF16)
        parts = []
        for part in (head, tail):
            part = jnp.dot(pick_row, part, preferred_element_type=F32).astype(BF16)
            parts.append(jnp.dot(part, pick_col, preferred_element_type=F32))
        wts[pl.ds(32 * m, 32), :] = jnp.where(col < 64, parts[0], parts[1]).astype(BF16)

    upper = lax.broadcasted_iota(jnp.int32, (8, LZ), 0) < 4

    def put_column(at, tile):
        both = jnp.where(upper, tile, pltpu.roll(pltpu.roll(tile, LZ - 1, 1), 4, 0))
        head = both.astype(BF16).astype(F32)
        xb[at] = jnp.concatenate([head, both - head], axis=0).astype(BF16)

    def own_columns(x, carry):
        for y in range(LY):
            put_column((x + 1) * EY + y + 1, nat[pl.ds(x * LY + y, 8, stride=NODES), :])
        return carry

    lax.fori_loop(0, LX, own_columns, 0)

    pl.semaphore_wait(barrier, nx * ny - 1 + nz - 1)

    def top_send(i):
        size, own, at = stages[i]

        def one(j, carry):
            pltpu.make_async_remote_copy(
                src_ref=tops.at[i, own],
                dst_ref=tops.at[i, own],
                send_sem=ms.at[i],
                recv_sem=mr.at[i],
                device_id=at(lax.rem(own + far_first(j, size), size)),
                device_id_type=MESH,
            ).start()
            return carry

        lax.fori_loop(1, size, one, 0)

    def top_wait(i, sem):
        rows = tops.at[i, pl.ds(0, stages[i][0] - 1)]
        pltpu.make_async_copy(rows, rows, sem.at[i]).wait()

    def top_gather(i):
        top_wait(i, mr)
        return jnp.max(tops[i, pl.ds(0, stages[i][0])], axis=0)

    def top_pass(i):
        tops[i + 1, stages[i + 1][1]] = top_gather(i)
        top_send(i + 1)


    def halo(src, dst, first, opposite, count, device, d, recv, rows=None):
        slot = d if recv else opposite
        span = None if rows is None else rows[1 - d if recv else d]
        part = (lambda ref, i: ref.at[i]) if rows is None else (lambda ref, i: ref.at[i, pl.ds(*span)])
        return pltpu.make_async_remote_copy(
            src_ref=part(src, d),
            dst_ref=part(dst, slot),
            send_sem=ss.at[first + d],
            recv_sem=rs.at[first + slot],
            device_id=device,
            device_id_type=MESH,
        )

    def group(has, src, dst, first, devices, rows=None):
        count = len(has)
        return [
            (
                has[d],
                functools.partial(halo, src, dst, first, count - 1 - d, count, devices[d], d, False, rows),
                functools.partial(halo, src, dst, first, count - 1 - d, count, devices[d], d, True, rows),
            )
            for d in range(count)
        ]

    temp_x = group(has_x, sx, rx, 0, step_x, ((TEMP * LY, LY),) * 2)
    temp_y = group(has_y, sy, ry, 2, step_y, ((TEMP * LX, LX),) * 2)
    temp_z = group(has_z, stz, rtz, 4, step_z)
    state_x = group(has_x, sx, rx, 6, step_x, ((0, 4 * LY), (0, 5 * LY)))
    state_y = group(has_y, sy, ry, 8, step_y, ((0, 4 * LX), (0, 5 * LX)))
    rate_x = group(has_x, sx, rx, 10, step_x, ((RATE * LY, LY),) * 2)
    rate_y = group(has_y, sy, ry, 12, step_y, ((RATE * LX, LX),) * 2)
    edges = group(has_e, se, re, 14, step_e)
    planes = group(has_z, sp, rp, 18, step_z)

    def start(copies):
        for has, send, _ in copies:

            @pl.when(has)
            def _():
                send().start()

    def wait(copies):
        for has, _, recv in copies:

            @pl.when(has)
            def _():
                recv().wait_recv()

    def sent(copies):
        for has, send, _ in copies:

            @pl.when(has)
            def _():
                send().wait_send()

    start(temp_y + temp_x + temp_z)
    top_send(0)

    start(state_y + state_x)

    w = wts[...]

    def cell_matrix(x, y):
        a = xb[pl.ds(x * EY + y, 2)].reshape(32, LZ)
        b = xb[pl.ds((x + 1) * EY + y, 2)].reshape(32, LZ)
        return jnp.concatenate([a, b, a, b], axis=0)

    def middle(x, w):
        for y in range(1, LY, 2):
            pair = [cell_matrix(x, y)]
            if y + 1 < LY:
                pair.append(cell_matrix(x, y + 1))
            got = jnp.dot(w, jnp.concatenate(pair, axis=1), preferred_element_type=F32)
            for k in range(len(pair)):
                f[x * CY + y + k] = got[:, k * LZ : (k + 1) * LZ]

    def sides(x, present):
        pair = [
            jnp.where(jnp.logical_and(present, has_y[d]), cell_matrix(x, (0, LY)[d]), jnp.zeros((128, LZ), BF16))
            for d in range(2)
        ]
        got = jnp.dot(w, jnp.concatenate(pair, axis=1), preferred_element_type=F32)
        for k in range(2):
            f[x * CY + (0, LY)[k]] = got[:, k * LZ : (k + 1) * LZ]

    def inner_row(x, carry):
        middle(x, w)
        return carry

    lax.fori_loop(1, 5, inner_row, 0)

    wait(temp_y + temp_x + temp_z)

    def border(dst, field):
        for x in range(LX):
            dst[pl.ds((x + 1) * TR + 8, LY), :] = nat[pl.ds(field * NODES + x * LY, LY), :]

    def border_faces(dst, field, sides):
        for d in sides:
            dst[pl.ds((0, EX - 1)[d] * TR + 8, LY), :] = rx[d, pl.ds(field * LY, LY), :]
            dst[pl.ds(TR + (7, 8 + LY)[d], LX, stride=TR), :] = ry[d, pl.ds(field * LX, LX), :]

    def border_edges(dst, field, which):
        for e in which:
            at = (0, EX - 1)[e // 2] * TR + (7, 8 + LY)[e % 2]
            dst[pl.ds(at, 1), :] = re[e, pl.ds(field, 1), :]

    border(te, TEMP)
    border_faces(te, TEMP, (0, 1))
    for x in range(LX):
        for h in range(2):
            j = 2 * x + h
            at = (x + 1) * TR + 8 + 8 * h
            centre = te[pl.ds(at, 8), :]
            plus_x, minus_x = te[pl.ds(at + TR, 8), :], te[pl.ds(at - TR, 8), :]
            plus_y, minus_y = te[pl.ds(at + 1, 8), :], te[pl.ds(at - 1, 8), :]
            from_low = rtz[0] if j == 1 else pltpu.roll(rtz[0], (1 - j) % LZ, 1)
            from_high = pltpu.roll(rtz[1], LZ - 1 - j, 1)
            minus_z = jnp.where(lane == 0, from_low, pltpu.roll(centre, 1, 1))
            plus_z = jnp.where(lane == LZ - 1, from_high, pltpu.roll(centre, LZ - 1, 1))
            laplace = plus_x + minus_x + plus_y + minus_y + plus_z + minus_z - 6.0 * centre
            v = [vel[pl.ds(k * NODES + j * 8, 8), :] for k in range(3)]
            transport = (
                v[0] * (plus_x - minus_x) + v[1] * (plus_y - minus_y) + v[2] * (plus_z - minus_z)
            )
            nat[pl.ds(RATE * NODES + j * 8, 8), :] = laplace - 0.5 * transport
    r0 = RATE * NODES
    for d in range(2):
        xs, ys = (0, LX - 1)[d], (0, LY - 1)[d]
        sx[d, pl.ds(RATE * LY, LY), :] = nat[pl.ds(r0 + xs * LY, LY), :]
        sy[d, pl.ds(RATE * LX, LX), :] = nat[pl.ds(r0 + ys, LX, stride=LY), :]
    for e in range(4):
        at = (0, LX - 1)[e // 2] * LY + (0, LY - 1)[e % 2]
        se[e] = nat[pl.ds(at, 8, stride=NODES), :]
    start(rate_y + rate_x + edges)
    lax.fori_loop(5, LX, inner_row, 0)
    top_pass(0)

    def plane_row(tiles, first):
        low = jnp.zeros((8, LZ), F32)
        high = jnp.zeros((8, LZ), F32)
        for k, tile in enumerate(tiles):
            y = first + k
            r = pltpu.roll(tile, y, 1) if y else tile
            low = jnp.where(lane == y, r, low)
            high = jnp.where(lane == (y - 1) % LZ, r, high)
        return low, pltpu.roll(high, 1, 1)

    def add_plane(x, low, high):
        for i, part in enumerate((low, high)):
            wide = jnp.concatenate([part, jnp.zeros((8, PW - LZ), F32)], axis=1)
            sp[i] = sp[i] + pltpu.roll(wide, x * EY, 1)

    sp[...] = jnp.zeros((2, 8, PW), F32)

    def own_plane(x, carry):
        tiles = [nat[pl.ds(x * LY + y, 8, stride=NODES), :] for y in range(LY)]
        add_plane(x + 1, *plane_row(tiles, 1))
        return carry

    lax.fori_loop(0, LX, own_plane, 0)

    wait(state_y + state_x + rate_y + rate_x + edges)
    for d in range(2):
        x = (0, EX - 1)[d]
        tiles = [re[2 * d]]
        tiles += [rx[d, pl.ds(y, 8, stride=LY), :] for y in range(LY)]
        tiles += [re[2 * d + 1]]
        for y in range(EY):
            put_column(x * EY + y, tiles[y])
        add_plane(x, *plane_row(tiles, 0))

    def side_columns(x, carry):
        low_tile = ry[0, pl.ds(x, 8, stride=LX), :]
        high_tile = ry[1, pl.ds(x, 8, stride=LX), :]
        put_column((x + 1) * EY, low_tile)
        put_column((x + 1) * EY + EY - 1, high_tile)
        a = plane_row([low_tile], 0)
        b = plane_row([high_tile], EY - 1)
        add_plane(x + 1, a[0] + b[0], a[1] + b[1])
        return carry

    lax.fori_loop(0, LX, side_columns, 0)
    start(planes)

    for x in range(1, LX):
        sides(x, True)
    for d in range(2):
        x = (0, LX)[d]
        middle(x, jnp.where(has_x[d], w, jnp.zeros((96, 128), BF16)))
        sides(x, has_x[d])

    def rows_at(x, y, m, q):
        return f[(x + 1 - (q >> 1)) * CY + y + 1 - (q & 1), pl.ds(32 * m + 8 * q, 8), :]

    def fixed_row(x, carry):
        for y in range(LY):
            f2[x * LY + y] = sum(rows_at(x, y, 2, q) for q in range(4))
        return carry

    lax.fori_loop(0, LX, fixed_row, 0)

    border_edges(te, TEMP, range(4))
    border(ge, RATE)
    border_faces(ge, RATE, (0, 1))
    border_edges(ge, RATE, range(4))
    border(ce, COEF)
    border_faces(ce, COEF, (0,))
    border_edges(ce, COEF, (0,))

    for i, ref in enumerate((te, ge)):
        for x in range(CX):
            total = ref[pl.ds(x * TR, TR), :] + ref[pl.ds((x + 1) * TR, TR), :]
            total = total + pltpu.roll(total, LZ - 1, 1)
            total = total + pltpu.roll(total, TR - 1, 0)
            sums[i, x] = total[:24]

    wait(planes)

    def shifted(a, q, back):
        by = EY * (q >> 1) + (q & 1)
        by = by if back else (PW - by) % PW
        return pltpu.roll(a, by, 1) if by else a

    place = lanes((8, PW))
    place_x = (place * 3641) >> 16
    place_y = place - EY * place_x
    outside = jnp.logical_or(
        jnp.logical_or(
            jnp.logical_and(place_x == 0, jnp.logical_not(has_x[0])),
            jnp.logical_and(place_x == LX, jnp.logical_not(has_x[1])),
        ),
        jnp.logical_or(
            jnp.logical_and(place_y == 0, jnp.logical_not(has_y[0])),
            jnp.logical_and(place_y == LY, jnp.logical_not(has_y[1])),
        ),
    )
    upper_wide = lax.broadcasted_iota(jnp.int32, (8, PW), 0) < 4
    for i in range(2):
        below, above = (rp[0], sp[0]) if i == 0 else (sp[1], rp[1])
        both = jnp.where(upper_wide, below, pltpu.roll(above, 4, 0))
        both = jnp.where(has_z[i], both, jnp.zeros((8, PW), F32))
        columns = []
        for q in range(4):
            part = jnp.where(outside, 0.0, shifted(both, q, False))
            head = part.astype(BF16).astype(F32)
            columns.append(jnp.concatenate([head, part - head], axis=0).astype(BF16))
        fp[i] = jnp.dot(w, jnp.concatenate(columns + columns, axis=0), preferred_element_type=F32)
        total = below + above
        total = sum(shifted(total, q, False) for q in range(4))
        ends[i] = total
        ends[i, pl.ds(COEF, 1), :] = below[COEF : COEF + 1]

    speed[...] = jnp.broadcast_to(jnp.max(top_gather(1), axis=1, keepdims=True), (8, LZ))
    locals_[6].wait()

    for i in range(2):
        top_wait(i, ms)
    sent(temp_x + temp_y + temp_z + state_x + state_y + rate_x + rate_y + edges + planes)


def finish(
    nat,
    mk,
    f,
    f2,
    fp,
    sums,
    ce,
    ends,
    speed,
    out_t,
    out_r,
    vis,
    nod,
    zp,
    lat,
    res,
    osem,
):
    t0, r0 = TEMP * NODES, RATE * NODES
    lane = lanes((8, LZ))
    upper_wide = lax.broadcasted_iota(jnp.int32, (8, PW), 0) < 4

    def shifted(a, q, back):
        by = EY * (q >> 1) + (q & 1)
        by = by if back else (PW - by) % PW
        return pltpu.roll(a, by, 1) if by else a

    def rows_at(x, y, m, q):
        return f[(x + 1 - (q >> 1)) * CY + y + 1 - (q & 1), pl.ds(32 * m + 8 * q, 8), :]

    step = 0.5 / (speed[0:1, :] + 6.0)
    step_wide = 0.5 / (speed[0:1, 0:1] + 6.0)

    for j in range(NODES // 8):
        lat[pl.ds(j * 8, 8), :] = (
            nat[pl.ds(t0 + j * 8, 8), :] + step * nat[pl.ds(r0 + j * 8, 8), :]
        )

    put_t = pltpu.make_async_copy(lat, out_t, osem.at[0])
    put_t.start()
    for x in range(CX):
        total = sums[0, x] + step * sums[1, x]
        viscosity = ce[pl.ds(x * TR, 24), :] * jnp.exp(1.5 - 0.375 * total)
        vis[0, x] = viscosity
        vis[1, x] = 0.25 / viscosity

    forces = []
    for i in range(2):
        coefficient = ends[i, pl.ds(COEF, 1), :]
        temp, change = ends[i, pl.ds(TEMP, 1), :], ends[i, pl.ds(RATE, 1), :]
        viscosity = coefficient * jnp.exp(1.5 - 0.375 * (temp + step_wide * change))
        stabilize = 0.25 / viscosity
        forces.append(
            viscosity * fp[i, pl.ds(0, 32), :]
            + stabilize * fp[i, pl.ds(32, 32), :]
            + fp[i, pl.ds(64, 32), :]
        )
    last = sum(
        shifted(jnp.where(upper_wide, forces[1][8 * q : 8 * q + 8], forces[0][8 * q : 8 * q + 8]), q, True)
        for q in range(4)
    )
    zp[...] = last

    is_last = lane == LZ - 1

    def node_row(x, carry):
        ends_row = pltpu.roll(zp[...], PW - EY * (x + 1), 1)[:, :LZ]
        for y in range(LY):
            total = f2[x * LY + y]
            for q in range(4):
                cell_x, cell_y = x + 1 - (q >> 1), y + 1 - (q & 1)
                viscosity = vis[0, cell_x, pl.ds(7 + cell_y, 1), :]
                stabilize = vis[1, cell_x, pl.ds(7 + cell_y, 1), :]
                total = total + viscosity * rows_at(x, y, 0, q) + stabilize * rows_at(x, y, 1, q)
            total = jnp.where(is_last, pltpu.roll(ends_row, LZ - 2 - y, 1), total)
            nod[pl.ds(y * 8, 8), :] = total
        for h in range(2):
            at = pl.multiple_of(x * LY + 8 * h, 8)
            flags = mk[pl.ds(at, 8), :]
            for c in range(4):
                near = nod[pl.ds(64 * h + c, 8, stride=8), :]
                far = nod[pl.ds(64 * h + 4 + c, 8, stride=8), :]
                value = near + pltpu.roll(far, 1, 1)
                if c == 2:
                    value = value - 2.0 * lat[pl.ds(at, 8), :]
                state = nat[pl.ds(pl.multiple_of(c * NODES + at, 8), 8), :]
                res[c, pl.ds(at, 8), :] = jnp.where((flags & (1 << c)) != 0, state, value)
        return carry

    puts = [put_t]
    for h in range(2):
        lax.fori_loop(h * LX // 2, (h + 1) * LX // 2, node_row, 0)
        part = pl.ds(h * NODES // 2, NODES // 2)
        puts.append(pltpu.make_async_copy(res.at[:, part], out_r.at[:, part], osem.at[1 + h]))
        puts[-1].start()
    for put in puts:
        put.wait()


def solution(mesh):
    sizes = nx, ny, nz = tuple(mesh.shape[a] for a in ("gx", "gy", "gz"))
    vmem = pltpu.VMEM
    hbm_spec = pl.BlockSpec(memory_space=pltpu.HBM)
    vmem_spec = pl.BlockSpec(memory_space=vmem)

    def in_hbm(a):
        return pltpu.with_memory_space_constraint(a, pltpu.HBM)

    def shards(heat, rate, guess, rock, mask, rheo, ops):
        kept = pl.pallas_call(
            functools.partial(exchange, sizes),
            out_shape=(
                vmem((8 * NODES, LZ), F32),
                vmem((NODES, LZ), jnp.int32),
                vmem((CX * CY, 96, LZ), F32),
                vmem((NODES, 8, LZ), F32),
                vmem((2, 96, PW), F32),
                vmem((2, CX, 24, LZ), F32),
                vmem((EX * TR, LZ), F32),
                vmem((2, 8, PW), F32),
                vmem((8, LZ), F32),
            ),
            in_specs=[hbm_spec] * 7,
            out_specs=[vmem_spec] * 9,
            scratch_shapes=[
                pltpu.SMEM((4,), F32),
                vmem((3, 32, 32), F32),
                vmem((3 * NODES, LZ), F32),
                vmem((NODES, LZ), jnp.int32),
                vmem((EX * TR, LZ), F32),
                vmem((EX * TR, LZ), F32),
                vmem((2, 8 * LY, LZ), F32),
                vmem((2, 8 * LY, LZ), F32),
                vmem((2, 8 * LX, LZ), F32),
                vmem((2, 8 * LX, LZ), F32),
                vmem((4, 8, LZ), F32),
                vmem((4, 8, LZ), F32),
                vmem((2, 8, LZ), F32),
                vmem((2, 8, LZ), F32),
                vmem((2, 8, PW), F32),
                vmem((2, 8, PW), F32),
                vmem((2, max(nx * ny, nz), 1, LZ), F32),
                vmem((EX * EY, 16, LZ), BF16),
                vmem((96, 128), BF16),
                pltpu.SemaphoreType.DMA((7,)),
                pltpu.SemaphoreType.DMA((20,)),
                pltpu.SemaphoreType.DMA((20,)),
                pltpu.SemaphoreType.DMA((2,)),
                pltpu.SemaphoreType.DMA((2,)),
            ],
            compiler_params=pltpu.CompilerParams(
                collective_id=0, has_side_effects=True, vmem_limit_bytes=24 * 1024 * 1024
            ),
        )(
            in_hbm(rheo),
            in_hbm(ops),
            in_hbm(heat.reshape(NODES, LZ)),
            in_hbm(rate.reshape(3 * NODES, LZ)),
            in_hbm(guess.reshape(4 * NODES, LZ)),
            in_hbm(rock.reshape(NODES, LZ)),
            in_hbm(mask.reshape(NODES, LZ)),
        )
        out_t, out_r = pl.pallas_call(
            finish,
            out_shape=(pltpu.HBM((NODES, LZ), F32), pltpu.HBM((4, NODES, LZ), F32)),
            in_specs=[vmem_spec] * 9,
            out_specs=[hbm_spec] * 2,
            scratch_shapes=[
                vmem((2, CX, 24, LZ), F32),
                vmem((8 * LY, LZ), F32),
                vmem((8, PW), F32),
                vmem((NODES, LZ), F32),
                vmem((4, NODES, LZ), F32),
                pltpu.SemaphoreType.DMA((3,)),
            ],
            compiler_params=pltpu.CompilerParams(vmem_limit_bytes=24 * 1024 * 1024),
        )(*(pltpu.with_memory_space_constraint(a, vmem) for a in kept))
        return out_t.reshape(LX, LY, LZ), out_r.reshape(4, LX, LY, LZ)

    grid = P("gx", "gy", "gz")
    fields = P(None, "gx", "gy", "gz")
    return jax.shard_map(
        shards,
        mesh=mesh,
        in_specs=(grid, fields, fields, grid, grid, P(), P()),
        out_specs=(grid, fields),
        check_vma=False,
    )
```

```python
import functools

import jax
import jax.numpy as jnp
from jax import lax
from jax.experimental import pallas as pl
from jax.experimental.pallas import tpu as pltpu
from jax.sharding import PartitionSpec as P

MESH = pl.DeviceIdType.MESH
F32 = jnp.float32
BF16 = jnp.bfloat16

LX, LY, LZ = 8, 16, 128
NODES = LX * LY
EX, EY = LX + 2, LY + 2
CX, CY = LX + 1, LY + 1
TR = 32
PW = 256
COEF, TEMP, RATE = 4, 5, 6


def lanes(shape):
    return lax.broadcasted_iota(jnp.int32, shape, 1)


def exchange(
    sizes,
    rheo_in,
    ops_in,
    heat,
    rate,
    guess,
    rock,
    mask,
    nat,
    mk,
    f,
    f2,
    fp,
    sums,
    ce,
    ends,
    speed,
    rheo,
    ops,
    vel,
    rk,
    te,
    ge,
    sx,
    rx,
    sy,
    ry,
    se,
    re,
    stz,
    rtz,
    sp,
    rp,
    tops,
    xb,
    wts,
    lsem,
    ss,
    rs,
    ms,
    mr,
):
    nx, ny, nz = sizes
    gx, gy, gz = lax.axis_index("gx"), lax.axis_index("gy"), lax.axis_index("gz")
    has_x = (gx > 0, gx < nx - 1)
    has_y = (gy > 0, gy < ny - 1)
    has_z = (gz > 0, gz < nz - 1)

    barrier = pltpu.get_barrier_semaphore()

    stages = (
        (nx * ny, gy * nx + gx, lambda t: {"gx": lax.rem(t, nx), "gy": t // nx}),
        (nz, gz, lambda t: {"gz": t}),
    )
    step_x = ({"gx": gx - 1}, {"gx": gx + 1})
    step_y = ({"gy": gy - 1}, {"gy": gy + 1})
    step_z = ({"gz": gz - 1}, {"gz": gz + 1})
    step_e = [dict(**step_x[e // 2], **step_y[e % 2]) for e in range(4)]
    has_e = [jnp.logical_and(has_x[e // 2], has_y[e % 2]) for e in range(4)]

    def greet(device):
        pl.semaphore_signal(barrier, inc=1, device_id=device, device_id_type=MESH)

    def far_first(j, size):
        return 1 + lax.rem(j - 1 + size // 2, max(size - 1, 1))

    for size, own, at in stages:

        def greet_one(j, carry):
            greet(at(lax.rem(own + far_first(j, size), size)))
            return carry

        lax.fori_loop(1, size, greet_one, 0)

    locals_ = [
        pltpu.make_async_copy(rate, vel, lsem.at[0]),
        pltpu.make_async_copy(heat, nat.at[pl.ds(TEMP * NODES, NODES)], lsem.at[1]),
        pltpu.make_async_copy(guess, nat.at[pl.ds(0, 4 * NODES)], lsem.at[2]),
        pltpu.make_async_copy(rock, rk, lsem.at[3]),
        pltpu.make_async_copy(rheo_in, rheo, lsem.at[4]),
        pltpu.make_async_copy(ops_in, ops, lsem.at[5]),
        pltpu.make_async_copy(mask, mk, lsem.at[6]),
    ]
    for copy in locals_:
        copy.start()

    for d in range(2):

        @pl.when(jnp.logical_not(has_x[d]))
        def _():
            rx[d] = jnp.zeros((8 * LY, LZ), F32)
            rx[d, pl.ds(COEF * LY, LY), :] = jnp.ones((LY, LZ), F32)

        @pl.when(jnp.logical_not(has_y[d]))
        def _():
            ry[d] = jnp.zeros((8 * LX, LZ), F32)
            ry[d, pl.ds(COEF * LX, LX), :] = jnp.ones((LX, LZ), F32)

        @pl.when(jnp.logical_not(has_z[d]))
        def _():
            rtz[d] = jnp.zeros((8, LZ), F32)
            rp[d] = jnp.where(
                lax.broadcasted_iota(jnp.int32, (8, PW), 0) == COEF, 1.0, 0.0
            ).astype(F32)

    for e in range(4):

        @pl.when(jnp.logical_not(has_e[e]))
        def _():
            re[e] = jnp.where(
                lax.broadcasted_iota(jnp.int32, (8, LZ), 0) == COEF, 1.0, 0.0
            ).astype(F32)

    nat[pl.ds(7 * NODES, NODES), :] = jnp.zeros((NODES, LZ), F32)

    locals_[0].wait()
    top = jnp.abs(vel[pl.ds(0, 8), :])

    def top_step(i, top):
        for k in range(8):
            top = jnp.maximum(top, jnp.abs(vel[pl.ds(pl.multiple_of(i * 64 + k * 8, 8), 8), :]))
        return top

    top = lax.fori_loop(0, 3 * NODES // 64, top_step, top)
    tops[0, stages[0][1]] = jnp.max(top, axis=0, keepdims=True)

    locals_[1].wait()
    lane = lanes((8, LZ))
    t0 = TEMP * NODES
    for d in range(2):
        xs, ys = (0, LX - 1)[d], (0, LY - 1)[d]
        sx[d, pl.ds(TEMP * LY, LY), :] = nat[pl.ds(t0 + xs * LY, LY), :]
        sy[d, pl.ds(TEMP * LX, LX), :] = nat[pl.ds(t0 + ys, LX, stride=LY), :]
    low = jnp.zeros((8, LZ), F32)
    high = jnp.zeros((8, LZ), F32)
    for j in range(NODES // 8):
        r = nat[pl.ds(t0 + j * 8, 8), :]
        if j:
            r = pltpu.roll(r, j, 1)
        low = jnp.where(lane == j, r, low)
        high = jnp.where(lane == (j - 1) % LZ, r, high)
    stz[0] = low
    stz[1] = high

    locals_[2].wait()
    locals_[3].wait()
    locals_[4].wait()

    for i in range(NODES // 8):
        label = rk[pl.ds(i * 8, 8), :]
        total = jnp.zeros((8, LZ), F32)
        for k in range(4):
            total = total + jnp.where(label == k, rheo[k], 0.0)
        nat[pl.ds(COEF * NODES + i * 8, 8), :] = total
    for d in range(2):
        xs, ys = (0, LX - 1)[d], (0, LY - 1)[d]
        for k in range(5):
            sx[d, pl.ds(k * LY, LY), :] = nat[pl.ds(k * NODES + xs * LY, LY), :]
            sy[d, pl.ds(k * LX, LX), :] = nat[pl.ds(k * NODES + ys, LX, stride=LY), :]
    pl.semaphore_wait(barrier, nx * ny - 1 + nz - 1)

    def top_send(i):
        size, own, at = stages[i]

        def one(j, carry):
            pltpu.make_async_remote_copy(
                src_ref=tops.at[i, own],
                dst_ref=tops.at[i, own],
                send_sem=ms.at[i],
                recv_sem=mr.at[i],
                device_id=at(lax.rem(own + far_first(j, size), size)),
                device_id_type=MESH,
            ).start()
            return carry

        lax.fori_loop(1, size, one, 0)

    def top_wait(i, sem):
        rows = tops.at[i, pl.ds(0, stages[i][0] - 1)]
        pltpu.make_async_copy(rows, rows, sem.at[i]).wait()

    def top_gather(i):
        top_wait(i, mr)
        return jnp.max(tops[i, pl.ds(0, stages[i][0])], axis=0)

    def top_pass(i):
        tops[i + 1, stages[i + 1][1]] = top_gather(i)
        top_send(i + 1)


    def halo(src, dst, first, opposite, count, device, d, recv, rows=None):
        slot = d if recv else opposite
        span = None if rows is None else rows[1 - d if recv else d]
        part = (lambda ref, i: ref.at[i]) if rows is None else (lambda ref, i: ref.at[i, pl.ds(*span)])
        return pltpu.make_async_remote_copy(
            src_ref=part(src, d),
            dst_ref=part(dst, slot),
            send_sem=ss.at[first + d],
            recv_sem=rs.at[first + slot],
            device_id=device,
            device_id_type=MESH,
        )

    def group(has, src, dst, first, devices, rows=None):
        count = len(has)
        return [
            (
                has[d],
                functools.partial(halo, src, dst, first, count - 1 - d, count, devices[d], d, False, rows),
                functools.partial(halo, src, dst, first, count - 1 - d, count, devices[d], d, True, rows),
            )
            for d in range(count)
        ]

    temp_x = group(has_x, sx, rx, 0, step_x, ((TEMP * LY, LY),) * 2)
    temp_y = group(has_y, sy, ry, 2, step_y, ((TEMP * LX, LX),) * 2)
    temp_z = group(has_z, stz, rtz, 4, step_z)
    state_x = group(has_x, sx, rx, 6, step_x, ((0, 4 * LY), (0, 5 * LY)))
    state_y = group(has_y, sy, ry, 8, step_y, ((0, 4 * LX), (0, 5 * LX)))
    rate_x = group(has_x, sx, rx, 10, step_x, ((RATE * LY, LY),) * 2)
    rate_y = group(has_y, sy, ry, 12, step_y, ((RATE * LX, LX),) * 2)
    edges = group(has_e, se, re, 14, step_e)
    planes = group(has_z, sp, rp, 18, step_z)

    def start(copies):
        for has, send, _ in copies:

            @pl.when(has)
            def _():
                send().start()

    def wait(copies):
        for has, _, recv in copies:

            @pl.when(has)
            def _():
                recv().wait_recv()

    def sent(copies):
        for has, send, _ in copies:

            @pl.when(has)
            def _():
                send().wait_send()

    start(temp_y + temp_x + temp_z)
    top_send(0)

    start(state_y + state_x)

    row = lax.broadcasted_iota(jnp.int32, (32, 32), 0)
    col = lax.broadcasted_iota(jnp.int32, (32, 32), 1)
    from_row = 8 * (row & 3) + 2 * (row >> 3) + ((row >> 2) & 1)
    pick_row = jnp.where(col == from_row, 1.0, 0.0).astype(BF16)
    row = lax.broadcasted_iota(jnp.int32, (32, 128), 0)
    col = lax.broadcasted_iota(jnp.int32, (32, 128), 1)
    from_col = 8 * (col & 3) + 2 * ((col >> 4) & 3) + ((col >> 2) & 1)
    pick_col = jnp.where(row == from_col, 1.0, 0.0).astype(BF16)
    locals_[5].wait()
    for m in range(3):
        block = ops[m]
        head = block.astype(BF16)
        tail = (block - head.astype(F32)).astype(BF16)
        parts = []
        for part in (head, tail):
            part = jnp.dot(pick_row, part, preferred_element_type=F32).astype(BF16)
            parts.append(jnp.dot(part, pick_col, preferred_element_type=F32))
        wts[pl.ds(32 * m, 32), :] = jnp.where(col < 64, parts[0], parts[1]).astype(BF16)

    upper = lax.broadcasted_iota(jnp.int32, (8, LZ), 0) < 4

    def put_column(at, tile):
        both = jnp.where(upper, tile, pltpu.roll(pltpu.roll(tile, LZ - 1, 1), 4, 0))
        head = both.astype(BF16).astype(F32)
        xb[at] = jnp.concatenate([head, both - head], axis=0).astype(BF16)

    def own_columns(x, carry):
        for y in range(LY):
            put_column((x + 1) * EY + y + 1, nat[pl.ds(x * LY + y, 8, stride=NODES), :])
        return carry

    lax.fori_loop(0, LX, own_columns, 0)

    w = wts[...]

    def cell_matrix(x, y):
        a = xb[pl.ds(x * EY + y, 2)].reshape(32, LZ)
        b = xb[pl.ds((x + 1) * EY + y, 2)].reshape(32, LZ)
        return jnp.concatenate([a, b, a, b], axis=0)

    def middle(x, w):
        for y in range(1, LY, 2):
            pair = [cell_matrix(x, y)]
            if y + 1 < LY:
                pair.append(cell_matrix(x, y + 1))
            got = jnp.dot(w, jnp.concatenate(pair, axis=1), preferred_element_type=F32)
            for k in range(len(pair)):
                f[x * CY + y + k] = got[:, k * LZ : (k + 1) * LZ]

    def sides(x, present):
        pair = [
            jnp.where(jnp.logical_and(present, has_y[d]), cell_matrix(x, (0, LY)[d]), jnp.zeros((128, LZ), BF16))
            for d in range(2)
        ]
        got = jnp.dot(w, jnp.concatenate(pair, axis=1), preferred_element_type=F32)
        for k in range(2):
            f[x * CY + (0, LY)[k]] = got[:, k * LZ : (k + 1) * LZ]

    def inner_row(x, carry):
        middle(x, w)
        return carry

    lax.fori_loop(1, 3, inner_row, 0)

    wait(temp_y + temp_x + temp_z)

    def border(dst, field):
        for x in range(LX):
            dst[pl.ds((x + 1) * TR + 8, LY), :] = nat[pl.ds(field * NODES + x * LY, LY), :]

    def border_faces(dst, field, sides):
        for d in sides:
            dst[pl.ds((0, EX - 1)[d] * TR + 8, LY), :] = rx[d, pl.ds(field * LY, LY), :]
            dst[pl.ds(TR + (7, 8 + LY)[d], LX, stride=TR), :] = ry[d, pl.ds(field * LX, LX), :]

    def border_edges(dst, field, which):
        for e in which:
            at = (0, EX - 1)[e // 2] * TR + (7, 8 + LY)[e % 2]
            dst[pl.ds(at, 1), :] = re[e, pl.ds(field, 1), :]

    border(te, TEMP)
    border_faces(te, TEMP, (0, 1))
    for x in range(LX):
        for h in range(2):
            j = 2 * x + h
            at = (x + 1) * TR + 8 + 8 * h
            centre = te[pl.ds(at, 8), :]
            plus_x, minus_x = te[pl.ds(at + TR, 8), :], te[pl.ds(at - TR, 8), :]
            plus_y, minus_y = te[pl.ds(at + 1, 8), :], te[pl.ds(at - 1, 8), :]
            from_low = rtz[0] if j == 1 else pltpu.roll(rtz[0], (1 - j) % LZ, 1)
            from_high = pltpu.roll(rtz[1], LZ - 1 - j, 1)
            minus_z = jnp.where(lane == 0, from_low, pltpu.roll(centre, 1, 1))
            plus_z = jnp.where(lane == LZ - 1, from_high, pltpu.roll(centre, LZ - 1, 1))
            laplace = plus_x + minus_x + plus_y + minus_y + plus_z + minus_z - 6.0 * centre
            v = [vel[pl.ds(k * NODES + j * 8, 8), :] for k in range(3)]
            transport = (
                v[0] * (plus_x - minus_x) + v[1] * (plus_y - minus_y) + v[2] * (plus_z - minus_z)
            )
            nat[pl.ds(RATE * NODES + j * 8, 8), :] = laplace - 0.5 * transport
    r0 = RATE * NODES
    for d in range(2):
        xs, ys = (0, LX - 1)[d], (0, LY - 1)[d]
        sx[d, pl.ds(RATE * LY, LY), :] = nat[pl.ds(r0 + xs * LY, LY), :]
        sy[d, pl.ds(RATE * LX, LX), :] = nat[pl.ds(r0 + ys, LX, stride=LY), :]
    for e in range(4):
        at = (0, LX - 1)[e // 2] * LY + (0, LY - 1)[e % 2]
        se[e] = nat[pl.ds(at, 8, stride=NODES), :]
    start(rate_y + edges + rate_x)
    lax.fori_loop(3, LX, inner_row, 0)
    top_pass(0)

    def plane_row(tiles, first):
        low = jnp.zeros((8, LZ), F32)
        high = jnp.zeros((8, LZ), F32)
        for k, tile in enumerate(tiles):
            y = first + k
            r = pltpu.roll(tile, y, 1) if y else tile
            low = jnp.where(lane == y, r, low)
            high = jnp.where(lane == (y - 1) % LZ, r, high)
        return low, pltpu.roll(high, 1, 1)

    def add_plane(x, low, high):
        for i, part in enumerate((low, high)):
            wide = jnp.concatenate([part, jnp.zeros((8, PW - LZ), F32)], axis=1)
            sp[i] = sp[i] + pltpu.roll(wide, x * EY, 1)

    sp[...] = jnp.zeros((2, 8, PW), F32)

    def own_plane(x, carry):
        tiles = [nat[pl.ds(x * LY + y, 8, stride=NODES), :] for y in range(LY)]
        add_plane(x + 1, *plane_row(tiles, 1))
        return carry

    lax.fori_loop(0, LX, own_plane, 0)

    wait(state_y + state_x + rate_y + rate_x + edges)
    ring = []
    for d in range(2):
        x = (0, EX - 1)[d]
        ring.append((x, 0, functools.partial(lambda e: re[e], 2 * d)))
        for y in range(LY):
            ring.append((x, y + 1, functools.partial(lambda d, y: rx[d, pl.ds(y, 8, stride=LY), :], d, y)))
        ring.append((x, EY - 1, functools.partial(lambda e: re[e], 2 * d + 1)))
    for x in range(LX):
        for d in range(2):
            ring.append(
                (x + 1, (0, EY - 1)[d], functools.partial(lambda d, x: ry[d, pl.ds(x, 8, stride=LX), :], d, x))
            )
    halves = [[jnp.zeros((8, LZ), F32) for _ in range(PW // LZ)] for _ in range(2)]
    for x, y, tile in ring:
        at = x * EY + y
        r = tile()
        if at % LZ:
            r = pltpu.roll(r, at % LZ, 1)
        for i in range(2):
            to = (at - i) % PW
            halves[i][to // LZ] = jnp.where(lane == to % LZ, r, halves[i][to // LZ])
    sp[0] = sp[0] + jnp.concatenate(halves[0], axis=1)
    sp[1] = sp[1] + pltpu.roll(jnp.concatenate(halves[1], axis=1), 1, 1)
    start(planes)

    for x, y, tile in ring:
        put_column(x * EY + y, tile())

    for x in range(1, LX):
        sides(x, True)
    for d in range(2):
        x = (0, LX)[d]
        middle(x, jnp.where(has_x[d], w, jnp.zeros((96, 128), BF16)))
        sides(x, has_x[d])

    def rows_at(x, y, m, q):
        return f[(x + 1 - (q >> 1)) * CY + y + 1 - (q & 1), pl.ds(32 * m + 8 * q, 8), :]

    def fixed_row(x, carry):
        for y in range(LY):
            f2[x * LY + y] = sum(rows_at(x, y, 2, q) for q in range(4))
        return carry

    lax.fori_loop(0, LX, fixed_row, 0)

    border_edges(te, TEMP, range(4))
    border(ge, RATE)
    border_faces(ge, RATE, (0, 1))
    border_edges(ge, RATE, range(4))
    border(ce, COEF)
    border_faces(ce, COEF, (0,))
    border_edges(ce, COEF, (0,))

    for i, ref in enumerate((te, ge)):
        for x in range(CX):
            total = ref[pl.ds(x * TR, TR), :] + ref[pl.ds((x + 1) * TR, TR), :]
            total = total + pltpu.roll(total, LZ - 1, 1)
            total = total + pltpu.roll(total, TR - 1, 0)
            sums[i, x] = total[:24]

    top_wait(0, ms)
    sent(temp_x + temp_y + temp_z + state_x + state_y + rate_x + rate_y + edges)
    wait(planes)

    def shifted(a, q, back):
        by = EY * (q >> 1) + (q & 1)
        by = by if back else (PW - by) % PW
        return pltpu.roll(a, by, 1) if by else a

    place = lanes((8, PW))
    place_x = (place * 3641) >> 16
    place_y = place - EY * place_x
    outside = jnp.logical_or(
        jnp.logical_or(
            jnp.logical_and(place_x == 0, jnp.logical_not(has_x[0])),
            jnp.logical_and(place_x == LX, jnp.logical_not(has_x[1])),
        ),
        jnp.logical_or(
            jnp.logical_and(place_y == 0, jnp.logical_not(has_y[0])),
            jnp.logical_and(place_y == LY, jnp.logical_not(has_y[1])),
        ),
    )
    upper_wide = lax.broadcasted_iota(jnp.int32, (8, PW), 0) < 4
    for i in range(2):
        below, above = (rp[0], sp[0]) if i == 0 else (sp[1], rp[1])
        both = jnp.where(upper_wide, below, pltpu.roll(above, 4, 0))
        both = jnp.where(has_z[i], both, jnp.zeros((8, PW), F32))
        columns = []
        for q in range(4):
            part = jnp.where(outside, 0.0, shifted(both, q, False))
            head = part.astype(BF16).astype(F32)
            columns.append(jnp.concatenate([head, part - head], axis=0).astype(BF16))
        fp[i] = jnp.dot(w, jnp.concatenate(columns + columns, axis=0), preferred_element_type=F32)
        total = below + above
        total = sum(shifted(total, q, False) for q in range(4))
        ends[i] = total
        ends[i, pl.ds(COEF, 1), :] = below[COEF : COEF + 1]

    speed[...] = jnp.broadcast_to(jnp.max(top_gather(1), axis=1, keepdims=True), (8, LZ))
    locals_[6].wait()

    top_wait(1, ms)
    sent(planes)


def finish(
    nat,
    mk,
    f,
    f2,
    fp,
    sums,
    ce,
    ends,
    speed,
    out_t,
    out_r,
    vis,
    nod,
    zp,
    lat,
    res,
    osem,
):
    t0, r0 = TEMP * NODES, RATE * NODES
    lane = lanes((8, LZ))
    upper_wide = lax.broadcasted_iota(jnp.int32, (8, PW), 0) < 4

    def shifted(a, q, back):
        by = EY * (q >> 1) + (q & 1)
        by = by if back else (PW - by) % PW
        return pltpu.roll(a, by, 1) if by else a

    def rows_at(x, y, m, q):
        return f[(x + 1 - (q >> 1)) * CY + y + 1 - (q & 1), pl.ds(32 * m + 8 * q, 8), :]

    step = 0.5 / (speed[0:1, :] + 6.0)
    step_wide = 0.5 / (speed[0:1, 0:1] + 6.0)

    for j in range(NODES // 8):
        lat[pl.ds(j * 8, 8), :] = (
            nat[pl.ds(t0 + j * 8, 8), :] + step * nat[pl.ds(r0 + j * 8, 8), :]
        )

    put_t = pltpu.make_async_copy(lat, out_t, osem.at[0])
    put_t.start()
    for x in range(CX):
        total = sums[0, x] + step * sums[1, x]
        viscosity = ce[pl.ds(x * TR, 24), :] * jnp.exp(1.5 - 0.375 * total)
        vis[0, x] = viscosity
        vis[1, x] = 0.25 / viscosity

    forces = []
    for i in range(2):
        coefficient = ends[i, pl.ds(COEF, 1), :]
        temp, change = ends[i, pl.ds(TEMP, 1), :], ends[i, pl.ds(RATE, 1), :]
        viscosity = coefficient * jnp.exp(1.5 - 0.375 * (temp + step_wide * change))
        stabilize = 0.25 / viscosity
        forces.append(
            viscosity * fp[i, pl.ds(0, 32), :]
            + stabilize * fp[i, pl.ds(32, 32), :]
            + fp[i, pl.ds(64, 32), :]
        )
    last = sum(
        shifted(jnp.where(upper_wide, forces[1][8 * q : 8 * q + 8], forces[0][8 * q : 8 * q + 8]), q, True)
        for q in range(4)
    )
    zp[...] = last

    is_last = lane == LZ - 1

    def node_row(x, carry):
        ends_row = pltpu.roll(zp[...], PW - EY * (x + 1), 1)[:, :LZ]
        for y in range(LY):
            total = f2[x * LY + y]
            for q in range(4):
                cell_x, cell_y = x + 1 - (q >> 1), y + 1 - (q & 1)
                viscosity = vis[0, cell_x, pl.ds(7 + cell_y, 1), :]
                stabilize = vis[1, cell_x, pl.ds(7 + cell_y, 1), :]
                total = total + viscosity * rows_at(x, y, 0, q) + stabilize * rows_at(x, y, 1, q)
            total = jnp.where(is_last, pltpu.roll(ends_row, LZ - 2 - y, 1), total)
            nod[pl.ds(y * 8, 8), :] = total
        for h in range(2):
            at = pl.multiple_of(x * LY + 8 * h, 8)
            flags = mk[pl.ds(at, 8), :]
            for c in range(4):
                near = nod[pl.ds(64 * h + c, 8, stride=8), :]
                far = nod[pl.ds(64 * h + 4 + c, 8, stride=8), :]
                value = near + pltpu.roll(far, 1, 1)
                if c == 2:
                    value = value - 2.0 * lat[pl.ds(at, 8), :]
                state = nat[pl.ds(pl.multiple_of(c * NODES + at, 8), 8), :]
                res[c, pl.ds(at, 8), :] = jnp.where((flags & (1 << c)) != 0, state, value)
        return carry

    puts = [put_t]
    for h in range(2):
        lax.fori_loop(h * LX // 2, (h + 1) * LX // 2, node_row, 0)
        part = pl.ds(h * NODES // 2, NODES // 2)
        puts.append(pltpu.make_async_copy(res.at[:, part], out_r.at[:, part], osem.at[1 + h]))
        puts[-1].start()
    for put in puts:
        put.wait()


def solution(mesh):
    sizes = nx, ny, nz = tuple(mesh.shape[a] for a in ("gx", "gy", "gz"))
    vmem = pltpu.VMEM
    hbm_spec = pl.BlockSpec(memory_space=pltpu.HBM)
    vmem_spec = pl.BlockSpec(memory_space=vmem)

    def in_hbm(a):
        return pltpu.with_memory_space_constraint(a, pltpu.HBM)

    def shards(heat, rate, guess, rock, mask, rheo, ops):
        kept = pl.pallas_call(
            functools.partial(exchange, sizes),
            out_shape=(
                vmem((8 * NODES, LZ), F32),
                vmem((NODES, LZ), jnp.int32),
                vmem((CX * CY, 96, LZ), F32),
                vmem((NODES, 8, LZ), F32),
                vmem((2, 96, PW), F32),
                vmem((2, CX, 24, LZ), F32),
                vmem((EX * TR, LZ), F32),
                vmem((2, 8, PW), F32),
                vmem((8, LZ), F32),
            ),
            in_specs=[hbm_spec] * 7,
            out_specs=[vmem_spec] * 9,
            scratch_shapes=[
                pltpu.SMEM((4,), F32),
                vmem((3, 32, 32), F32),
                vmem((3 * NODES, LZ), F32),
                vmem((NODES, LZ), jnp.int32),
                vmem((EX * TR, LZ), F32),
                vmem((EX * TR, LZ), F32),
                vmem((2, 8 * LY, LZ), F32),
                vmem((2, 8 * LY, LZ), F32),
                vmem((2, 8 * LX, LZ), F32),
                vmem((2, 8 * LX, LZ), F32),
                vmem((4, 8, LZ), F32),
                vmem((4, 8, LZ), F32),
                vmem((2, 8, LZ), F32),
                vmem((2, 8, LZ), F32),
                vmem((2, 8, PW), F32),
                vmem((2, 8, PW), F32),
                vmem((2, max(nx * ny, nz), 1, LZ), F32),
                vmem((EX * EY, 16, LZ), BF16),
                vmem((96, 128), BF16),
                pltpu.SemaphoreType.DMA((7,)),
                pltpu.SemaphoreType.DMA((20,)),
                pltpu.SemaphoreType.DMA((20,)),
                pltpu.SemaphoreType.DMA((2,)),
                pltpu.SemaphoreType.DMA((2,)),
            ],
            compiler_params=pltpu.CompilerParams(
                collective_id=0, has_side_effects=True, vmem_limit_bytes=24 * 1024 * 1024
            ),
        )(
            in_hbm(rheo),
            in_hbm(ops),
            in_hbm(heat.reshape(NODES, LZ)),
            in_hbm(rate.reshape(3 * NODES, LZ)),
            in_hbm(guess.reshape(4 * NODES, LZ)),
            in_hbm(rock.reshape(NODES, LZ)),
            in_hbm(mask.reshape(NODES, LZ)),
        )
        out_t, out_r = pl.pallas_call(
            finish,
            out_shape=(pltpu.HBM((NODES, LZ), F32), pltpu.HBM((4, NODES, LZ), F32)),
            in_specs=[vmem_spec] * 9,
            out_specs=[hbm_spec] * 2,
            scratch_shapes=[
                vmem((2, CX, 24, LZ), F32),
                vmem((8 * LY, LZ), F32),
                vmem((8, PW), F32),
                vmem((NODES, LZ), F32),
                vmem((4, NODES, LZ), F32),
                pltpu.SemaphoreType.DMA((3,)),
            ],
            compiler_params=pltpu.CompilerParams(vmem_limit_bytes=24 * 1024 * 1024),
        )(*(pltpu.with_memory_space_constraint(a, vmem) for a in kept))
        return out_t.reshape(LX, LY, LZ), out_r.reshape(4, LX, LY, LZ)

    grid = P("gx", "gy", "gz")
    fields = P(None, "gx", "gy", "gz")
    return jax.shard_map(
        shards,
        mesh=mesh,
        in_specs=(grid, fields, fields, grid, grid, P(), P()),
        out_specs=(grid, fields),
        check_vma=False,
    )
```

```python
import functools

import jax
import jax.numpy as jnp
from jax import lax
from jax.experimental import pallas as pl
from jax.experimental.pallas import tpu as pltpu
from jax.sharding import PartitionSpec as P

MESH = pl.DeviceIdType.MESH
F32 = jnp.float32
BF16 = jnp.bfloat16

LX, LY, LZ = 8, 16, 128
NODES = LX * LY
EX, EY = LX + 2, LY + 2
CX, CY = LX + 1, LY + 1
TR = 32
PW = 256
COEF, TEMP, RATE = 4, 5, 6


def lanes(shape):
    return lax.broadcasted_iota(jnp.int32, shape, 1)


def exchange(
    sizes,
    rheo_in,
    ops_in,
    heat,
    rate,
    guess,
    rock,
    mask,
    nat,
    mk,
    f,
    f2,
    fp,
    sums,
    ce,
    ends,
    speed,
    rheo,
    ops,
    vel,
    rk,
    te,
    ge,
    sx,
    rx,
    sy,
    ry,
    se,
    re,
    rgx,
    rgy,
    stz,
    rtz,
    sp,
    rp,
    tops,
    xb,
    wts,
    lsem,
    ss,
    rs,
    ms,
    mr,
):
    nx, ny, nz = sizes
    gx, gy, gz = lax.axis_index("gx"), lax.axis_index("gy"), lax.axis_index("gz")
    has_x = (gx > 0, gx < nx - 1)
    has_y = (gy > 0, gy < ny - 1)
    has_z = (gz > 0, gz < nz - 1)

    locals_ = [
        pltpu.make_async_copy(rate, vel, lsem.at[0]),
        pltpu.make_async_copy(heat, nat.at[pl.ds(TEMP * NODES, NODES)], lsem.at[1]),
        pltpu.make_async_copy(guess, nat.at[pl.ds(0, 4 * NODES)], lsem.at[2]),
        pltpu.make_async_copy(rock, rk, lsem.at[3]),
        pltpu.make_async_copy(rheo_in, rheo, lsem.at[4]),
        pltpu.make_async_copy(ops_in, ops, lsem.at[5]),
        pltpu.make_async_copy(mask, mk, lsem.at[6]),
    ]
    for copy in locals_[:2]:
        copy.start()

    barrier = pltpu.get_barrier_semaphore()

    stages = (
        (nx * ny, gy * nx + gx, lambda t: {"gx": lax.rem(t, nx), "gy": t // nx}),
        (nz, gz, lambda t: {"gz": t}),
    )
    step_x = ({"gx": gx - 1}, {"gx": gx + 1})
    step_y = ({"gy": gy - 1}, {"gy": gy + 1})
    step_z = ({"gz": gz - 1}, {"gz": gz + 1})
    step_e = [dict(**step_x[e // 2], **step_y[e % 2]) for e in range(4)]
    has_e = [jnp.logical_and(has_x[e // 2], has_y[e % 2]) for e in range(4)]

    def greet(device):
        pl.semaphore_signal(barrier, inc=1, device_id=device, device_id_type=MESH)

    def far_first(j, size):
        return 1 + lax.rem(j - 1 + size // 2, max(size - 1, 1))

    for size, own, at in stages:

        def greet_one(j, carry):
            greet(at(lax.rem(own + far_first(j, size), size)))
            return carry

        lax.fori_loop(1, size, greet_one, 0)

    for copy in locals_[2:]:
        copy.start()

    for d in range(2):

        @pl.when(jnp.logical_not(has_x[d]))
        def _():
            rx[d] = jnp.zeros((8 * LY, LZ), F32)
            rgx[d] = jnp.zeros((LY, LZ), F32)
            rx[d, pl.ds(COEF * LY, LY), :] = jnp.ones((LY, LZ), F32)

        @pl.when(jnp.logical_not(has_y[d]))
        def _():
            ry[d] = jnp.zeros((8 * LX, LZ), F32)
            rgy[d] = jnp.zeros((LX, LZ), F32)
            ry[d, pl.ds(COEF * LX, LX), :] = jnp.ones((LX, LZ), F32)

        @pl.when(jnp.logical_not(has_z[d]))
        def _():
            rtz[d] = jnp.zeros((8, LZ), F32)
            rp[d] = jnp.where(
                lax.broadcasted_iota(jnp.int32, (8, PW), 0) == COEF, 1.0, 0.0
            ).astype(F32)

    for e in range(4):

        @pl.when(jnp.logical_not(has_e[e]))
        def _():
            re[e] = jnp.where(
                lax.broadcasted_iota(jnp.int32, (8, LZ), 0) == COEF, 1.0, 0.0
            ).astype(F32)

    nat[pl.ds(7 * NODES, NODES), :] = jnp.zeros((NODES, LZ), F32)

    locals_[0].wait()
    top = jnp.abs(vel[pl.ds(0, 8), :])

    def top_step(i, top):
        for k in range(8):
            top = jnp.maximum(top, jnp.abs(vel[pl.ds(pl.multiple_of(i * 64 + k * 8, 8), 8), :]))
        return top

    top = lax.fori_loop(0, 3 * NODES // 64, top_step, top)
    tops[0, stages[0][1]] = jnp.max(top, axis=0, keepdims=True)

    locals_[1].wait()
    lane = lanes((8, LZ))
    t0 = TEMP * NODES
    for d in range(2):
        xs, ys = (0, LX - 1)[d], (0, LY - 1)[d]
        sx[d, pl.ds(TEMP * LY, LY), :] = nat[pl.ds(t0 + xs * LY, LY), :]
        sy[d, pl.ds(TEMP * LX, LX), :] = nat[pl.ds(t0 + ys, LX, stride=LY), :]
    low = jnp.zeros((8, LZ), F32)
    high = jnp.zeros((8, LZ), F32)
    for j in range(NODES // 8):
        r = nat[pl.ds(t0 + j * 8, 8), :]
        if j:
            r = pltpu.roll(r, j, 1)
        low = jnp.where(lane == j, r, low)
        high = jnp.where(lane == (j - 1) % LZ, r, high)
    stz[0] = low
    stz[1] = high

    locals_[2].wait()
    locals_[3].wait()
    locals_[4].wait()

    for i in range(NODES // 8):
        label = rk[pl.ds(i * 8, 8), :]
        total = jnp.zeros((8, LZ), F32)
        for k in range(4):
            total = total + jnp.where(label == k, rheo[k], 0.0)
        nat[pl.ds(COEF * NODES + i * 8, 8), :] = total
    for d in range(2):
        xs, ys = (0, LX - 1)[d], (0, LY - 1)[d]
        for k in range(5):
            sx[d, pl.ds(k * LY, LY), :] = nat[pl.ds(k * NODES + xs * LY, LY), :]
            sy[d, pl.ds(k * LX, LX), :] = nat[pl.ds(k * NODES + ys, LX, stride=LY), :]
    pl.semaphore_wait(barrier, nx * ny - 1 + nz - 1)

    def top_send(i):
        size, own, at = stages[i]

        def one(j, carry):
            pltpu.make_async_remote_copy(
                src_ref=tops.at[i, own],
                dst_ref=tops.at[i, own],
                send_sem=ms.at[i],
                recv_sem=mr.at[i],
                device_id=at(lax.rem(own + far_first(j, size), size)),
                device_id_type=MESH,
            ).start()
            return carry

        lax.fori_loop(1, size, one, 0)

    def top_wait(i, sem):
        rows = tops.at[i, pl.ds(0, stages[i][0] - 1)]
        pltpu.make_async_copy(rows, rows, sem.at[i]).wait()

    def top_gather(i):
        top_wait(i, mr)
        return jnp.max(tops[i, pl.ds(0, stages[i][0])], axis=0)

    def top_pass(i):
        tops[i + 1, stages[i + 1][1]] = top_gather(i)
        top_send(i + 1)


    def halo(src, dst, first, opposite, count, device, d, recv, rows=None, whole=False):
        slot = d if recv else opposite
        span = None if rows is None else rows[1 - d if recv else d]

        def part(ref, i, whole):
            return ref.at[i] if whole else ref.at[i, pl.ds(*span)]

        return pltpu.make_async_remote_copy(
            src_ref=part(src, d, rows is None),
            dst_ref=part(dst, slot, rows is None or whole),
            send_sem=ss.at[first + d],
            recv_sem=rs.at[first + slot],
            device_id=device,
            device_id_type=MESH,
        )

    def group(has, src, dst, first, devices, rows=None, whole=False):
        count = len(has)
        return [
            (
                has[d],
                functools.partial(halo, src, dst, first, count - 1 - d, count, devices[d], d, False, rows, whole),
                functools.partial(halo, src, dst, first, count - 1 - d, count, devices[d], d, True, rows, whole),
            )
            for d in range(count)
        ]

    temp_x = group(has_x, sx, rx, 0, step_x, ((TEMP * LY, LY),) * 2)
    temp_y = group(has_y, sy, ry, 2, step_y, ((TEMP * LX, LX),) * 2)
    temp_z = group(has_z, stz, rtz, 4, step_z)
    state_x = group(has_x, sx, rx, 6, step_x, ((0, 4 * LY), (0, 5 * LY)))
    state_y = group(has_y, sy, ry, 8, step_y, ((0, 4 * LX), (0, 5 * LX)))
    rate_x = group(has_x, sx, rgx, 10, step_x, ((RATE * LY, LY),) * 2, True)
    rate_y = group(has_y, sy, rgy, 12, step_y, ((RATE * LX, LX),) * 2, True)
    edges = group(has_e, se, re, 14, step_e)
    planes = group(has_z, sp, rp, 18, step_z)

    def start(copies):
        for has, send, _ in copies:

            @pl.when(has)
            def _():
                send().start()

    def wait(copies):
        for has, _, recv in copies:

            @pl.when(has)
            def _():
                recv().wait_recv()

    def sent(copies):
        for has, send, _ in copies:

            @pl.when(has)
            def _():
                send().wait_send()

    start(temp_y + temp_x + temp_z)
    top_send(0)

    start(state_y + state_x)

    row = lax.broadcasted_iota(jnp.int32, (32, 32), 0)
    col = lax.broadcasted_iota(jnp.int32, (32, 32), 1)
    from_row = 8 * (row & 3) + 2 * (row >> 3) + ((row >> 2) & 1)
    pick_row = jnp.where(col == from_row, 1.0, 0.0).astype(BF16)
    row = lax.broadcasted_iota(jnp.int32, (32, 128), 0)
    col = lax.broadcasted_iota(jnp.int32, (32, 128), 1)
    from_col = 8 * (col & 3) + 2 * ((col >> 4) & 3) + ((col >> 2) & 1)
    pick_col = jnp.where(row == from_col, 1.0, 0.0).astype(BF16)
    locals_[5].wait()
    for m in range(3):
        block = ops[m]
        head = block.astype(BF16)
        tail = (block - head.astype(F32)).astype(BF16)
        parts = []
        for part in (head, tail):
            part = jnp.dot(pick_row, part, preferred_element_type=F32).astype(BF16)
            parts.append(jnp.dot(part, pick_col, preferred_element_type=F32))
        wts[pl.ds(32 * m, 32), :] = jnp.where(col < 64, parts[0], parts[1]).astype(BF16)

    upper = lax.broadcasted_iota(jnp.int32, (8, LZ), 0) < 4

    def put_column(at, tile):
        both = jnp.where(upper, tile, pltpu.roll(pltpu.roll(tile, LZ - 1, 1), 4, 0))
        head = both.astype(BF16).astype(F32)
        xb[at] = jnp.concatenate([head, both - head], axis=0).astype(BF16)

    def own_columns(x, carry):
        for y in range(LY):
            put_column((x + 1) * EY + y + 1, nat[pl.ds(x * LY + y, 8, stride=NODES), :])
        return carry

    lax.fori_loop(0, LX, own_columns, 0)

    w = wts[...]

    def cell_matrix(x, y):
        a = xb[pl.ds(x * EY + y, 2)].reshape(32, LZ)
        b = xb[pl.ds((x + 1) * EY + y, 2)].reshape(32, LZ)
        return jnp.concatenate([a, b, a, b], axis=0)

    def middle(x, w):
        for y in range(1, LY, 2):
            pair = [cell_matrix(x, y)]
            if y + 1 < LY:
                pair.append(cell_matrix(x, y + 1))
            got = jnp.dot(w, jnp.concatenate(pair, axis=1), preferred_element_type=F32)
            for k in range(len(pair)):
                f[x * CY + y + k] = got[:, k * LZ : (k + 1) * LZ]

    def sides(x, present):
        pair = [
            jnp.where(jnp.logical_and(present, has_y[d]), cell_matrix(x, (0, LY)[d]), jnp.zeros((128, LZ), BF16))
            for d in range(2)
        ]
        got = jnp.dot(w, jnp.concatenate(pair, axis=1), preferred_element_type=F32)
        for k in range(2):
            f[x * CY + (0, LY)[k]] = got[:, k * LZ : (k + 1) * LZ]

    def inner_row(x, carry):
        middle(x, w)
        return carry

    lax.fori_loop(1, 3, inner_row, 0)

    wait(temp_y + temp_x + temp_z)

    def border(dst, field):
        for x in range(LX):
            dst[pl.ds((x + 1) * TR + 8, LY), :] = nat[pl.ds(field * NODES + x * LY, LY), :]

    def border_faces(dst, field, sides):
        for d in sides:
            dst[pl.ds((0, EX - 1)[d] * TR + 8, LY), :] = rx[d, pl.ds(field * LY, LY), :]
            dst[pl.ds(TR + (7, 8 + LY)[d], LX, stride=TR), :] = ry[d, pl.ds(field * LX, LX), :]

    def border_edges(dst, field, which):
        for e in which:
            at = (0, EX - 1)[e // 2] * TR + (7, 8 + LY)[e % 2]
            dst[pl.ds(at, 1), :] = re[e, pl.ds(field, 1), :]

    border(te, TEMP)
    border_faces(te, TEMP, (0, 1))
    for x in range(LX):
        for h in range(2):
            j = 2 * x + h
            at = (x + 1) * TR + 8 + 8 * h
            centre = te[pl.ds(at, 8), :]
            plus_x, minus_x = te[pl.ds(at + TR, 8), :], te[pl.ds(at - TR, 8), :]
            plus_y, minus_y = te[pl.ds(at + 1, 8), :], te[pl.ds(at - 1, 8), :]
            from_low = rtz[0] if j == 1 else pltpu.roll(rtz[0], (1 - j) % LZ, 1)
            from_high = pltpu.roll(rtz[1], LZ - 1 - j, 1)
            minus_z = jnp.where(lane == 0, from_low, pltpu.roll(centre, 1, 1))
            plus_z = jnp.where(lane == LZ - 1, from_high, pltpu.roll(centre, LZ - 1, 1))
            laplace = plus_x + minus_x + plus_y + minus_y + plus_z + minus_z - 6.0 * centre
            v = [vel[pl.ds(k * NODES + j * 8, 8), :] for k in range(3)]
            transport = (
                v[0] * (plus_x - minus_x) + v[1] * (plus_y - minus_y) + v[2] * (plus_z - minus_z)
            )
            nat[pl.ds(RATE * NODES + j * 8, 8), :] = laplace - 0.5 * transport
    r0 = RATE * NODES
    for d in range(2):
        xs, ys = (0, LX - 1)[d], (0, LY - 1)[d]
        sx[d, pl.ds(RATE * LY, LY), :] = nat[pl.ds(r0 + xs * LY, LY), :]
        sy[d, pl.ds(RATE * LX, LX), :] = nat[pl.ds(r0 + ys, LX, stride=LY), :]
    for e in range(4):
        at = (0, LX - 1)[e // 2] * LY + (0, LY - 1)[e % 2]
        se[e] = nat[pl.ds(at, 8, stride=NODES), :]
    start(rate_y + edges + rate_x)
    lax.fori_loop(3, 5, inner_row, 0)
    top_pass(0)
    lax.fori_loop(5, LX, inner_row, 0)

    def plane_row(tiles, first):
        low = jnp.zeros((8, LZ), F32)
        high = jnp.zeros((8, LZ), F32)
        for k, tile in enumerate(tiles):
            y = first + k
            r = pltpu.roll(tile, y, 1) if y else tile
            low = jnp.where(lane == y, r, low)
            high = jnp.where(lane == (y - 1) % LZ, r, high)
        return low, pltpu.roll(high, 1, 1)

    def add_plane(x, low, high):
        for i, part in enumerate((low, high)):
            wide = jnp.concatenate([part, jnp.zeros((8, PW - LZ), F32)], axis=1)
            sp[i] = sp[i] + pltpu.roll(wide, x * EY, 1)

    sp[...] = jnp.zeros((2, 8, PW), F32)

    def own_plane(x, carry):
        tiles = [nat[pl.ds(x * LY + y, 8, stride=NODES), :] for y in range(LY)]
        add_plane(x + 1, *plane_row(tiles, 1))
        return carry

    lax.fori_loop(0, LX, own_plane, 0)

    ring = []
    for d in range(2):
        for y in range(LY):
            ring.append(
                ((0, EX - 1)[d], y + 1, functools.partial(lambda d, y: rx[d, pl.ds(y, 8, stride=LY), :], d, y))
            )
        for x in range(LX):
            ring.append(
                (x + 1, (0, EY - 1)[d], functools.partial(lambda d, x: ry[d, pl.ds(x, 8, stride=LX), :], d, x))
            )
    for e in range(4):
        ring.append(((0, EX - 1)[e // 2], (0, EY - 1)[e % 2], functools.partial(lambda e: re[e], e)))

    wait(state_y + state_x)
    for x, y, tile in ring[:-4]:
        put_column(x * EY + y, tile())
    for x in range(1, LX):
        sides(x, True)
    for d in range(2):
        middle((0, LX)[d], jnp.where(has_x[d], w, jnp.zeros((96, 128), BF16)))

    def rows_at(x, y, m, q):
        return f[(x + 1 - (q >> 1)) * CY + y + 1 - (q & 1), pl.ds(32 * m + 8 * q, 8), :]

    def fixed_row(x, carry):
        for y in range(LY):
            f2[x * LY + y] = sum(rows_at(x, y, 2, q) for q in range(4))
        return carry

    lax.fori_loop(1, LX - 1, fixed_row, 0)

    wait(rate_y + rate_x + edges)
    for d in range(2):
        rx[d, pl.ds(RATE * LY, LY), :] = rgx[d]
        ry[d, pl.ds(RATE * LX, LX), :] = rgy[d]
    halves = [[jnp.zeros((8, LZ), F32) for _ in range(PW // LZ)] for _ in range(2)]
    for x, y, tile in ring:
        at = x * EY + y
        r = tile()
        if at % LZ:
            r = pltpu.roll(r, at % LZ, 1)
        for i in range(2):
            to = (at - i) % PW
            halves[i][to // LZ] = jnp.where(lane == to % LZ, r, halves[i][to // LZ])
    sp[0] = sp[0] + jnp.concatenate(halves[0], axis=1)
    sp[1] = sp[1] + pltpu.roll(jnp.concatenate(halves[1], axis=1), 1, 1)
    start(planes)

    for x, y, tile in ring[-4:]:
        put_column(x * EY + y, tile())
    for d in range(2):
        sides((0, LX)[d], has_x[d])
    for x in (0, LX - 1):
        fixed_row(x, 0)

    border_edges(te, TEMP, range(4))
    border(ge, RATE)
    border_faces(ge, RATE, (0, 1))
    border_edges(ge, RATE, range(4))
    border(ce, COEF)
    border_faces(ce, COEF, (0,))
    border_edges(ce, COEF, (0,))

    for i, ref in enumerate((te, ge)):
        for x in range(CX):
            total = ref[pl.ds(x * TR, TR), :] + ref[pl.ds((x + 1) * TR, TR), :]
            total = total + pltpu.roll(total, LZ - 1, 1)
            total = total + pltpu.roll(total, TR - 1, 0)
            sums[i, x] = total[:24]

    top_wait(0, ms)
    sent(temp_x + temp_y + temp_z + state_x + state_y + rate_x + rate_y + edges)
    wait(planes)

    def shifted(a, q, back):
        by = EY * (q >> 1) + (q & 1)
        by = by if back else (PW - by) % PW
        return pltpu.roll(a, by, 1) if by else a

    place = lanes((8, PW))
    place_x = (place * 3641) >> 16
    place_y = place - EY * place_x
    outside = jnp.logical_or(
        jnp.logical_or(
            jnp.logical_and(place_x == 0, jnp.logical_not(has_x[0])),
            jnp.logical_and(place_x == LX, jnp.logical_not(has_x[1])),
        ),
        jnp.logical_or(
            jnp.logical_and(place_y == 0, jnp.logical_not(has_y[0])),
            jnp.logical_and(place_y == LY, jnp.logical_not(has_y[1])),
        ),
    )
    upper_wide = lax.broadcasted_iota(jnp.int32, (8, PW), 0) < 4
    for i in range(2):
        below, above = (rp[0], sp[0]) if i == 0 else (sp[1], rp[1])
        both = jnp.where(upper_wide, below, pltpu.roll(above, 4, 0))
        both = jnp.where(has_z[i], both, jnp.zeros((8, PW), F32))
        columns = []
        for q in range(4):
            part = jnp.where(outside, 0.0, shifted(both, q, False))
            head = part.astype(BF16).astype(F32)
            columns.append(jnp.concatenate([head, part - head], axis=0).astype(BF16))
        fp[i] = jnp.dot(w, jnp.concatenate(columns + columns, axis=0), preferred_element_type=F32)
        total = below + above
        total = sum(shifted(total, q, False) for q in range(4))
        ends[i] = total
        ends[i, pl.ds(COEF, 1), :] = below[COEF : COEF + 1]

    speed[...] = jnp.broadcast_to(jnp.max(top_gather(1), axis=1, keepdims=True), (8, LZ))
    locals_[6].wait()

    top_wait(1, ms)
    sent(planes)


def finish(
    nat,
    mk,
    f,
    f2,
    fp,
    sums,
    ce,
    ends,
    speed,
    out_t,
    out_r,
    vis,
    nod,
    zp,
    lat,
    res,
    osem,
):
    t0, r0 = TEMP * NODES, RATE * NODES
    lane = lanes((8, LZ))
    upper_wide = lax.broadcasted_iota(jnp.int32, (8, PW), 0) < 4

    def shifted(a, q, back):
        by = EY * (q >> 1) + (q & 1)
        by = by if back else (PW - by) % PW
        return pltpu.roll(a, by, 1) if by else a

    def rows_at(x, y, m, q):
        return f[(x + 1 - (q >> 1)) * CY + y + 1 - (q & 1), pl.ds(32 * m + 8 * q, 8), :]

    step = 0.5 / (speed[0:1, :] + 6.0)
    step_wide = 0.5 / (speed[0:1, 0:1] + 6.0)

    for j in range(NODES // 8):
        lat[pl.ds(j * 8, 8), :] = (
            nat[pl.ds(t0 + j * 8, 8), :] + step * nat[pl.ds(r0 + j * 8, 8), :]
        )

    put_t = pltpu.make_async_copy(lat, out_t, osem.at[0])
    put_t.start()
    for x in range(CX):
        total = sums[0, x] + step * sums[1, x]
        viscosity = ce[pl.ds(x * TR, 24), :] * jnp.exp(1.5 - 0.375 * total)
        vis[0, x] = viscosity
        vis[1, x] = 0.25 / viscosity

    forces = []
    for i in range(2):
        coefficient = ends[i, pl.ds(COEF, 1), :]
        temp, change = ends[i, pl.ds(TEMP, 1), :], ends[i, pl.ds(RATE, 1), :]
        viscosity = coefficient * jnp.exp(1.5 - 0.375 * (temp + step_wide * change))
        stabilize = 0.25 / viscosity
        forces.append(
            viscosity * fp[i, pl.ds(0, 32), :]
            + stabilize * fp[i, pl.ds(32, 32), :]
            + fp[i, pl.ds(64, 32), :]
        )
    last = sum(
        shifted(jnp.where(upper_wide, forces[1][8 * q : 8 * q + 8], forces[0][8 * q : 8 * q + 8]), q, True)
        for q in range(4)
    )
    zp[...] = last

    is_last = lane == LZ - 1

    def node_row(x, carry):
        ends_row = pltpu.roll(zp[...], PW - EY * (x + 1), 1)[:, :LZ]
        for y in range(LY):
            total = f2[x * LY + y]
            for q in range(4):
                cell_x, cell_y = x + 1 - (q >> 1), y + 1 - (q & 1)
                viscosity = vis[0, cell_x, pl.ds(7 + cell_y, 1), :]
                stabilize = vis[1, cell_x, pl.ds(7 + cell_y, 1), :]
                total = total + viscosity * rows_at(x, y, 0, q) + stabilize * rows_at(x, y, 1, q)
            total = jnp.where(is_last, pltpu.roll(ends_row, LZ - 2 - y, 1), total)
            nod[pl.ds(y * 8, 8), :] = total
        for h in range(2):
            at = pl.multiple_of(x * LY + 8 * h, 8)
            flags = mk[pl.ds(at, 8), :]
            for c in range(4):
                near = nod[pl.ds(64 * h + c, 8, stride=8), :]
                far = nod[pl.ds(64 * h + 4 + c, 8, stride=8), :]
                value = near + pltpu.roll(far, 1, 1)
                if c == 2:
                    value = value - 2.0 * lat[pl.ds(at, 8), :]
                state = nat[pl.ds(pl.multiple_of(c * NODES + at, 8), 8), :]
                res[c, pl.ds(at, 8), :] = jnp.where((flags & (1 << c)) != 0, state, value)
        return carry

    puts = [put_t]
    for h in range(2):
        lax.fori_loop(h * LX // 2, (h + 1) * LX // 2, node_row, 0)
        part = pl.ds(h * NODES // 2, NODES // 2)
        puts.append(pltpu.make_async_copy(res.at[:, part], out_r.at[:, part], osem.at[1 + h]))
        puts[-1].start()
    for put in puts:
        put.wait()


def solution(mesh):
    sizes = nx, ny, nz = tuple(mesh.shape[a] for a in ("gx", "gy", "gz"))
    vmem = pltpu.VMEM
    hbm_spec = pl.BlockSpec(memory_space=pltpu.HBM)
    vmem_spec = pl.BlockSpec(memory_space=vmem)

    def in_hbm(a):
        return pltpu.with_memory_space_constraint(a, pltpu.HBM)

    def shards(heat, rate, guess, rock, mask, rheo, ops):
        kept = pl.pallas_call(
            functools.partial(exchange, sizes),
            out_shape=(
                vmem((8 * NODES, LZ), F32),
                vmem((NODES, LZ), jnp.int32),
                vmem((CX * CY, 96, LZ), F32),
                vmem((NODES, 8, LZ), F32),
                vmem((2, 96, PW), F32),
                vmem((2, CX, 24, LZ), F32),
                vmem((EX * TR, LZ), F32),
                vmem((2, 8, PW), F32),
                vmem((8, LZ), F32),
            ),
            in_specs=[hbm_spec] * 7,
            out_specs=[vmem_spec] * 9,
            scratch_shapes=[
                pltpu.SMEM((4,), F32),
                vmem((3, 32, 32), F32),
                vmem((3 * NODES, LZ), F32),
                vmem((NODES, LZ), jnp.int32),
                vmem((EX * TR, LZ), F32),
                vmem((EX * TR, LZ), F32),
                vmem((2, 8 * LY, LZ), F32),
                vmem((2, 8 * LY, LZ), F32),
                vmem((2, 8 * LX, LZ), F32),
                vmem((2, 8 * LX, LZ), F32),
                vmem((4, 8, LZ), F32),
                vmem((4, 8, LZ), F32),
                vmem((2, LY, LZ), F32),
                vmem((2, LX, LZ), F32),
                vmem((2, 8, LZ), F32),
                vmem((2, 8, LZ), F32),
                vmem((2, 8, PW), F32),
                vmem((2, 8, PW), F32),
                vmem((2, max(nx * ny, nz), 1, LZ), F32),
                vmem((EX * EY, 16, LZ), BF16),
                vmem((96, 128), BF16),
                pltpu.SemaphoreType.DMA((7,)),
                pltpu.SemaphoreType.DMA((20,)),
                pltpu.SemaphoreType.DMA((20,)),
                pltpu.SemaphoreType.DMA((2,)),
                pltpu.SemaphoreType.DMA((2,)),
            ],
            compiler_params=pltpu.CompilerParams(
                collective_id=0, has_side_effects=True, vmem_limit_bytes=24 * 1024 * 1024
            ),
        )(
            in_hbm(rheo),
            in_hbm(ops),
            in_hbm(heat.reshape(NODES, LZ)),
            in_hbm(rate.reshape(3 * NODES, LZ)),
            in_hbm(guess.reshape(4 * NODES, LZ)),
            in_hbm(rock.reshape(NODES, LZ)),
            in_hbm(mask.reshape(NODES, LZ)),
        )
        out_t, out_r = pl.pallas_call(
            finish,
            out_shape=(pltpu.HBM((NODES, LZ), F32), pltpu.HBM((4, NODES, LZ), F32)),
            in_specs=[vmem_spec] * 9,
            out_specs=[hbm_spec] * 2,
            scratch_shapes=[
                vmem((2, CX, 24, LZ), F32),
                vmem((8 * LY, LZ), F32),
                vmem((8, PW), F32),
                vmem((NODES, LZ), F32),
                vmem((4, NODES, LZ), F32),
                pltpu.SemaphoreType.DMA((3,)),
            ],
            compiler_params=pltpu.CompilerParams(vmem_limit_bytes=24 * 1024 * 1024),
        )(*(pltpu.with_memory_space_constraint(a, vmem) for a in kept))
        return out_t.reshape(LX, LY, LZ), out_r.reshape(4, LX, LY, LZ)

    grid = P("gx", "gy", "gz")
    fields = P(None, "gx", "gy", "gz")
    return jax.shard_map(
        shards,
        mesh=mesh,
        in_specs=(grid, fields, fields, grid, grid, P(), P()),
        out_specs=(grid, fields),
        check_vma=False,
    )
```

```python
import functools

import jax
import jax.numpy as jnp
from jax import lax
from jax.experimental import pallas as pl
from jax.experimental.pallas import tpu as pltpu
from jax.sharding import PartitionSpec as P

MESH = pl.DeviceIdType.MESH
F32 = jnp.float32
BF16 = jnp.bfloat16

LX, LY, LZ = 8, 16, 128
NODES = LX * LY
EX, EY = LX + 2, LY + 2
CX, CY = LX + 1, LY + 1
TR = 32
PW = 256
COEF, TEMP, RATE = 4, 5, 6


def lanes(shape):
    return lax.broadcasted_iota(jnp.int32, shape, 1)


def exchange(
    sizes,
    rheo_in,
    ops_in,
    heat,
    rate,
    guess,
    rock,
    mask,
    nat,
    mk,
    f,
    f2,
    fp,
    sums,
    ce,
    ends,
    speed,
    rheo,
    ops,
    vel,
    rk,
    te,
    ge,
    sx,
    rx,
    sy,
    ry,
    se,
    re,
    rgx,
    rgy,
    stz,
    rtz,
    sp,
    rp,
    tops,
    xb,
    wts,
    lsem,
    ss,
    rs,
    ms,
    mr,
):
    nx, ny, nz = sizes
    gx, gy, gz = lax.axis_index("gx"), lax.axis_index("gy"), lax.axis_index("gz")
    has_x = (gx > 0, gx < nx - 1)
    has_y = (gy > 0, gy < ny - 1)
    has_z = (gz > 0, gz < nz - 1)

    locals_ = [
        pltpu.make_async_copy(rate, vel, lsem.at[0]),
        pltpu.make_async_copy(heat, nat.at[pl.ds(TEMP * NODES, NODES)], lsem.at[1]),
        pltpu.make_async_copy(guess, nat.at[pl.ds(0, 4 * NODES)], lsem.at[2]),
        pltpu.make_async_copy(rock, rk, lsem.at[3]),
        pltpu.make_async_copy(rheo_in, rheo, lsem.at[4]),
        pltpu.make_async_copy(ops_in, ops, lsem.at[5]),
        pltpu.make_async_copy(mask, mk, lsem.at[6]),
    ]
    for copy in locals_[:2]:
        copy.start()

    barrier = pltpu.get_barrier_semaphore()

    inner = min(nz, 8)
    gz_in, gz_out = lax.rem(gz, inner), gz // inner
    stages = (
        (nx * ny, gy * nx + gx, lambda t: {"gx": lax.rem(t, nx), "gy": t // nx}),
        (nz // inner, gz_out, lambda t: {"gz": t * inner + gz_in}),
        (inner, gz_in, lambda t: {"gz": gz_out * inner + t}),
    )
    step_x = ({"gx": gx - 1}, {"gx": gx + 1})
    step_y = ({"gy": gy - 1}, {"gy": gy + 1})
    step_z = ({"gz": gz - 1}, {"gz": gz + 1})
    step_e = [dict(**step_x[e // 2], **step_y[e % 2]) for e in range(4)]
    has_e = [jnp.logical_and(has_x[e // 2], has_y[e % 2]) for e in range(4)]

    def greet(device):
        pl.semaphore_signal(barrier, inc=1, device_id=device, device_id_type=MESH)

    def far_first(j, size):
        return 1 + lax.rem(j - 1 + size // 2, max(size - 1, 1))

    for size, own, at in stages:

        def greet_one(j, carry):
            greet(at(lax.rem(own + far_first(j, size), size)))
            return carry

        lax.fori_loop(1, size, greet_one, 0)

    greeted = sum(size - 1 for size, _, _ in stages)
    for d in range(2):

        @pl.when(has_z[d])
        def _():
            greet(step_z[d])

        greeted = greeted + has_z[d].astype(jnp.int32)

    for copy in locals_[2:]:
        copy.start()

    for d in range(2):

        @pl.when(jnp.logical_not(has_x[d]))
        def _():
            rx[d] = jnp.zeros((8 * LY, LZ), F32)
            rgx[d] = jnp.zeros((LY, LZ), F32)
            rx[d, pl.ds(COEF * LY, LY), :] = jnp.ones((LY, LZ), F32)

        @pl.when(jnp.logical_not(has_y[d]))
        def _():
            ry[d] = jnp.zeros((8 * LX, LZ), F32)
            rgy[d] = jnp.zeros((LX, LZ), F32)
            ry[d, pl.ds(COEF * LX, LX), :] = jnp.ones((LX, LZ), F32)

        @pl.when(jnp.logical_not(has_z[d]))
        def _():
            rtz[d] = jnp.zeros((8, LZ), F32)
            rp[d] = jnp.where(
                lax.broadcasted_iota(jnp.int32, (8, PW), 0) == COEF, 1.0, 0.0
            ).astype(F32)

    for e in range(4):

        @pl.when(jnp.logical_not(has_e[e]))
        def _():
            re[e] = jnp.where(
                lax.broadcasted_iota(jnp.int32, (8, LZ), 0) == COEF, 1.0, 0.0
            ).astype(F32)

    nat[pl.ds(7 * NODES, NODES), :] = jnp.zeros((NODES, LZ), F32)

    locals_[0].wait()
    top = jnp.abs(vel[pl.ds(0, 8), :])

    def top_step(i, top):
        for k in range(8):
            top = jnp.maximum(top, jnp.abs(vel[pl.ds(pl.multiple_of(i * 64 + k * 8, 8), 8), :]))
        return top

    top = lax.fori_loop(0, 3 * NODES // 64, top_step, top)
    tops[0, stages[0][1]] = jnp.max(top, axis=0, keepdims=True)

    locals_[1].wait()
    lane = lanes((8, LZ))
    t0 = TEMP * NODES
    for d in range(2):
        xs, ys = (0, LX - 1)[d], (0, LY - 1)[d]
        sx[d, pl.ds(TEMP * LY, LY), :] = nat[pl.ds(t0 + xs * LY, LY), :]
        sy[d, pl.ds(TEMP * LX, LX), :] = nat[pl.ds(t0 + ys, LX, stride=LY), :]
    low = jnp.zeros((8, LZ), F32)
    high = jnp.zeros((8, LZ), F32)
    for j in range(NODES // 8):
        r = nat[pl.ds(t0 + j * 8, 8), :]
        if j:
            r = pltpu.roll(r, j, 1)
        low = jnp.where(lane == j, r, low)
        high = jnp.where(lane == (j - 1) % LZ, r, high)
    stz[0] = low
    stz[1] = high

    pl.semaphore_wait(barrier, greeted)

    def top_send(i):
        size, own, at = stages[i]

        def one(j, carry):
            pltpu.make_async_remote_copy(
                src_ref=tops.at[i, own],
                dst_ref=tops.at[i, own],
                send_sem=ms.at[i],
                recv_sem=mr.at[i],
                device_id=at(lax.rem(own + far_first(j, size), size)),
                device_id_type=MESH,
            ).start()
            return carry

        lax.fori_loop(1, size, one, 0)

    def top_wait(i, sem):
        if stages[i][0] > 1:
            rows = tops.at[i, pl.ds(0, stages[i][0] - 1)]
            pltpu.make_async_copy(rows, rows, sem.at[i]).wait()

    def top_gather(i):
        top_wait(i, mr)
        return jnp.max(tops[i, pl.ds(0, stages[i][0])], axis=0)

    def top_pass(i):
        tops[i + 1, stages[i + 1][1]] = top_gather(i)
        top_send(i + 1)


    def halo(src, dst, first, opposite, count, device, d, recv, rows=None, whole=False):
        slot = d if recv else opposite
        span = None if rows is None else rows[1 - d if recv else d]

        def part(ref, i, whole):
            return ref.at[i] if whole else ref.at[i, pl.ds(*span)]

        return pltpu.make_async_remote_copy(
            src_ref=part(src, d, rows is None),
            dst_ref=part(dst, slot, rows is None or whole),
            send_sem=ss.at[first + d],
            recv_sem=rs.at[first + slot],
            device_id=device,
            device_id_type=MESH,
        )

    def group(has, src, dst, first, devices, rows=None, whole=False):
        count = len(has)
        return [
            (
                has[d],
                functools.partial(halo, src, dst, first, count - 1 - d, count, devices[d], d, False, rows, whole),
                functools.partial(halo, src, dst, first, count - 1 - d, count, devices[d], d, True, rows, whole),
            )
            for d in range(count)
        ]

    temp_x = group(has_x, sx, rx, 0, step_x, ((TEMP * LY, LY),) * 2)
    temp_y = group(has_y, sy, ry, 2, step_y, ((TEMP * LX, LX),) * 2)
    temp_z = group(has_z, stz, rtz, 4, step_z)
    state_x = group(has_x, sx, rx, 6, step_x, ((0, 4 * LY), (0, 5 * LY)))
    state_y = group(has_y, sy, ry, 8, step_y, ((0, 4 * LX), (0, 5 * LX)))
    rate_x = group(has_x, sx, rgx, 10, step_x, ((RATE * LY, LY),) * 2, True)
    rate_y = group(has_y, sy, rgy, 12, step_y, ((RATE * LX, LX),) * 2, True)
    edges = group(has_e, se, re, 14, step_e)
    planes = group(has_z, sp, rp, 18, step_z)

    def start(copies):
        for has, send, _ in copies:

            @pl.when(has)
            def _():
                send().start()

    def wait(copies):
        for has, _, recv in copies:

            @pl.when(has)
            def _():
                recv().wait_recv()

    def sent(copies):
        for has, send, _ in copies:

            @pl.when(has)
            def _():
                send().wait_send()

    top_send(0)
    start(temp_y + temp_x + temp_z)

    locals_[2].wait()
    locals_[3].wait()
    locals_[4].wait()

    for i in range(NODES // 8):
        label = rk[pl.ds(i * 8, 8), :]
        total = jnp.zeros((8, LZ), F32)
        for k in range(4):
            total = total + jnp.where(label == k, rheo[k], 0.0)
        nat[pl.ds(COEF * NODES + i * 8, 8), :] = total
    for d in range(2):
        xs, ys = (0, LX - 1)[d], (0, LY - 1)[d]
        for k in range(5):
            sx[d, pl.ds(k * LY, LY), :] = nat[pl.ds(k * NODES + xs * LY, LY), :]
            sy[d, pl.ds(k * LX, LX), :] = nat[pl.ds(k * NODES + ys, LX, stride=LY), :]

    start(state_y + state_x)

    row = lax.broadcasted_iota(jnp.int32, (32, 32), 0)
    col = lax.broadcasted_iota(jnp.int32, (32, 32), 1)
    from_row = 8 * (row & 3) + 2 * (row >> 3) + ((row >> 2) & 1)
    pick_row = jnp.where(col == from_row, 1.0, 0.0).astype(BF16)
    row = lax.broadcasted_iota(jnp.int32, (32, 128), 0)
    col = lax.broadcasted_iota(jnp.int32, (32, 128), 1)
    from_col = 8 * (col & 3) + 2 * ((col >> 4) & 3) + ((col >> 2) & 1)
    pick_col = jnp.where(row == from_col, 1.0, 0.0).astype(BF16)
    locals_[5].wait()
    for m in range(3):
        block = ops[m]
        head = block.astype(BF16)
        tail = (block - head.astype(F32)).astype(BF16)
        parts = []
        for part in (head, tail):
            part = jnp.dot(pick_row, part, preferred_element_type=F32).astype(BF16)
            parts.append(jnp.dot(part, pick_col, preferred_element_type=F32))
        wts[pl.ds(32 * m, 32), :] = jnp.where(col < 64, parts[0], parts[1]).astype(BF16)

    upper = lax.broadcasted_iota(jnp.int32, (8, LZ), 0) < 4

    def put_column(at, tile):
        both = jnp.where(upper, tile, pltpu.roll(pltpu.roll(tile, LZ - 1, 1), 4, 0))
        head = both.astype(BF16).astype(F32)
        xb[at] = jnp.concatenate([head, both - head], axis=0).astype(BF16)

    def own_columns(x, carry):
        for y in range(LY):
            put_column((x + 1) * EY + y + 1, nat[pl.ds(x * LY + y, 8, stride=NODES), :])
        return carry

    lax.fori_loop(0, LX, own_columns, 0)

    w = wts[...]

    def cell_matrix(x, y):
        a = xb[pl.ds(x * EY + y, 2)].reshape(32, LZ)
        b = xb[pl.ds((x + 1) * EY + y, 2)].reshape(32, LZ)
        return jnp.concatenate([a, b, a, b], axis=0)

    def middle(x, w):
        for y in range(1, LY, 2):
            pair = [cell_matrix(x, y)]
            if y + 1 < LY:
                pair.append(cell_matrix(x, y + 1))
            got = jnp.dot(w, jnp.concatenate(pair, axis=1), preferred_element_type=F32)
            for k in range(len(pair)):
                f[x * CY + y + k] = got[:, k * LZ : (k + 1) * LZ]

    def sides(x, present):
        pair = [
            jnp.where(jnp.logical_and(present, has_y[d]), cell_matrix(x, (0, LY)[d]), jnp.zeros((128, LZ), BF16))
            for d in range(2)
        ]
        got = jnp.dot(w, jnp.concatenate(pair, axis=1), preferred_element_type=F32)
        for k in range(2):
            f[x * CY + (0, LY)[k]] = got[:, k * LZ : (k + 1) * LZ]

    def inner_row(x, carry):
        middle(x, w)
        return carry

    lax.fori_loop(1, 3, inner_row, 0)

    wait(temp_y + temp_x + temp_z)

    def border(dst, field):
        for x in range(LX):
            dst[pl.ds((x + 1) * TR + 8, LY), :] = nat[pl.ds(field * NODES + x * LY, LY), :]

    def border_faces(dst, field, sides):
        for d in sides:
            dst[pl.ds((0, EX - 1)[d] * TR + 8, LY), :] = rx[d, pl.ds(field * LY, LY), :]
            dst[pl.ds(TR + (7, 8 + LY)[d], LX, stride=TR), :] = ry[d, pl.ds(field * LX, LX), :]

    def border_edges(dst, field, which):
        for e in which:
            at = (0, EX - 1)[e // 2] * TR + (7, 8 + LY)[e % 2]
            dst[pl.ds(at, 1), :] = re[e, pl.ds(field, 1), :]

    border(te, TEMP)
    border_faces(te, TEMP, (0, 1))
    for x in range(LX):
        for h in range(2):
            j = 2 * x + h
            at = (x + 1) * TR + 8 + 8 * h
            centre = te[pl.ds(at, 8), :]
            plus_x, minus_x = te[pl.ds(at + TR, 8), :], te[pl.ds(at - TR, 8), :]
            plus_y, minus_y = te[pl.ds(at + 1, 8), :], te[pl.ds(at - 1, 8), :]
            from_low = rtz[0] if j == 1 else pltpu.roll(rtz[0], (1 - j) % LZ, 1)
            from_high = pltpu.roll(rtz[1], LZ - 1 - j, 1)
            minus_z = jnp.where(lane == 0, from_low, pltpu.roll(centre, 1, 1))
            plus_z = jnp.where(lane == LZ - 1, from_high, pltpu.roll(centre, LZ - 1, 1))
            laplace = plus_x + minus_x + plus_y + minus_y + plus_z + minus_z - 6.0 * centre
            v = [vel[pl.ds(k * NODES + j * 8, 8), :] for k in range(3)]
            transport = (
                v[0] * (plus_x - minus_x) + v[1] * (plus_y - minus_y) + v[2] * (plus_z - minus_z)
            )
            nat[pl.ds(RATE * NODES + j * 8, 8), :] = laplace - 0.5 * transport
    r0 = RATE * NODES
    for d in range(2):
        xs, ys = (0, LX - 1)[d], (0, LY - 1)[d]
        sx[d, pl.ds(RATE * LY, LY), :] = nat[pl.ds(r0 + xs * LY, LY), :]
        sy[d, pl.ds(RATE * LX, LX), :] = nat[pl.ds(r0 + ys, LX, stride=LY), :]
    for e in range(4):
        at = (0, LX - 1)[e // 2] * LY + (0, LY - 1)[e % 2]
        se[e] = nat[pl.ds(at, 8, stride=NODES), :]
    start(rate_y + edges + rate_x)
    lax.fori_loop(3, 5, inner_row, 0)
    top_pass(0)
    lax.fori_loop(5, LX, inner_row, 0)

    def plane_row(tiles, first):
        low = jnp.zeros((8, LZ), F32)
        high = jnp.zeros((8, LZ), F32)
        for k, tile in enumerate(tiles):
            y = first + k
            r = pltpu.roll(tile, y, 1) if y else tile
            low = jnp.where(lane == y, r, low)
            high = jnp.where(lane == (y - 1) % LZ, r, high)
        return low, pltpu.roll(high, 1, 1)

    def add_plane(x, low, high):
        for i, part in enumerate((low, high)):
            wide = jnp.concatenate([part, jnp.zeros((8, PW - LZ), F32)], axis=1)
            sp[i] = sp[i] + pltpu.roll(wide, x * EY, 1)

    sp[...] = jnp.zeros((2, 8, PW), F32)

    def own_plane(x, carry):
        tiles = [nat[pl.ds(x * LY + y, 8, stride=NODES), :] for y in range(LY)]
        add_plane(x + 1, *plane_row(tiles, 1))
        return carry

    lax.fori_loop(0, LX, own_plane, 0)
    top_pass(1)

    ring = []
    for d in range(2):
        for y in range(LY):
            ring.append(
                ((0, EX - 1)[d], y + 1, functools.partial(lambda d, y: rx[d, pl.ds(y, 8, stride=LY), :], d, y))
            )
        for x in range(LX):
            ring.append(
                (x + 1, (0, EY - 1)[d], functools.partial(lambda d, x: ry[d, pl.ds(x, 8, stride=LX), :], d, x))
            )
    for e in range(4):
        ring.append(((0, EX - 1)[e // 2], (0, EY - 1)[e % 2], functools.partial(lambda e: re[e], e)))

    wait(state_y + state_x)
    for x, y, tile in ring[:-4]:
        put_column(x * EY + y, tile())
    for x in range(1, LX):
        sides(x, True)
    for d in range(2):
        middle((0, LX)[d], jnp.where(has_x[d], w, jnp.zeros((96, 128), BF16)))

    def rows_at(x, y, m, q):
        return f[(x + 1 - (q >> 1)) * CY + y + 1 - (q & 1), pl.ds(32 * m + 8 * q, 8), :]

    def fixed_row(x, carry):
        for y in range(LY):
            f2[x * LY + y] = sum(rows_at(x, y, 2, q) for q in range(4))
        return carry

    lax.fori_loop(1, LX - 1, fixed_row, 0)

    wait(rate_y + rate_x + edges)
    for d in range(2):
        rx[d, pl.ds(RATE * LY, LY), :] = rgx[d]
        ry[d, pl.ds(RATE * LX, LX), :] = rgy[d]
    halves = [[jnp.zeros((8, LZ), F32) for _ in range(PW // LZ)] for _ in range(2)]
    for x, y, tile in ring:
        at = x * EY + y
        r = tile()
        if at % LZ:
            r = pltpu.roll(r, at % LZ, 1)
        for i in range(2):
            to = (at - i) % PW
            halves[i][to // LZ] = jnp.where(lane == to % LZ, r, halves[i][to // LZ])
    sp[0] = sp[0] + jnp.concatenate(halves[0], axis=1)
    sp[1] = sp[1] + pltpu.roll(jnp.concatenate(halves[1], axis=1), 1, 1)
    start(planes)

    for x, y, tile in ring[-4:]:
        put_column(x * EY + y, tile())
    for d in range(2):
        sides((0, LX)[d], has_x[d])
    for x in (0, LX - 1):
        fixed_row(x, 0)

    border_edges(te, TEMP, range(4))
    border(ge, RATE)
    border_faces(ge, RATE, (0, 1))
    border_edges(ge, RATE, range(4))
    border(ce, COEF)
    border_faces(ce, COEF, (0,))
    border_edges(ce, COEF, (0,))

    for i, ref in enumerate((te, ge)):
        for x in range(CX):
            total = ref[pl.ds(x * TR, TR), :] + ref[pl.ds((x + 1) * TR, TR), :]
            total = total + pltpu.roll(total, LZ - 1, 1)
            total = total + pltpu.roll(total, TR - 1, 0)
            sums[i, x] = total[:24]

    top_wait(0, ms)
    top_wait(1, ms)
    sent(temp_x + temp_y + temp_z + state_x + state_y + rate_x + rate_y + edges)
    wait(planes)

    def shifted(a, q, back):
        by = EY * (q >> 1) + (q & 1)
        by = by if back else (PW - by) % PW
        return pltpu.roll(a, by, 1) if by else a

    place = lanes((8, PW))
    place_x = (place * 3641) >> 16
    place_y = place - EY * place_x
    outside = jnp.logical_or(
        jnp.logical_or(
            jnp.logical_and(place_x == 0, jnp.logical_not(has_x[0])),
            jnp.logical_and(place_x == LX, jnp.logical_not(has_x[1])),
        ),
        jnp.logical_or(
            jnp.logical_and(place_y == 0, jnp.logical_not(has_y[0])),
            jnp.logical_and(place_y == LY, jnp.logical_not(has_y[1])),
        ),
    )
    upper_wide = lax.broadcasted_iota(jnp.int32, (8, PW), 0) < 4
    for i in range(2):
        below, above = (rp[0], sp[0]) if i == 0 else (sp[1], rp[1])
        both = jnp.where(upper_wide, below, pltpu.roll(above, 4, 0))
        both = jnp.where(has_z[i], both, jnp.zeros((8, PW), F32))
        columns = []
        for q in range(4):
            part = jnp.where(outside, 0.0, shifted(both, q, False))
            head = part.astype(BF16).astype(F32)
            columns.append(jnp.concatenate([head, part - head], axis=0).astype(BF16))
        fp[i] = jnp.dot(w, jnp.concatenate(columns + columns, axis=0), preferred_element_type=F32)
        total = below + above
        total = sum(shifted(total, q, False) for q in range(4))
        ends[i] = total
        ends[i, pl.ds(COEF, 1), :] = below[COEF : COEF + 1]

    speed[...] = jnp.broadcast_to(jnp.max(top_gather(2), axis=1, keepdims=True), (8, LZ))
    locals_[6].wait()

    top_wait(2, ms)
    sent(planes)


def finish(
    nat,
    mk,
    f,
    f2,
    fp,
    sums,
    ce,
    ends,
    speed,
    out_t,
    out_r,
    vis,
    nod,
    zp,
    lat,
    res,
    osem,
):
    t0, r0 = TEMP * NODES, RATE * NODES
    lane = lanes((8, LZ))
    upper_wide = lax.broadcasted_iota(jnp.int32, (8, PW), 0) < 4

    def shifted(a, q, back):
        by = EY * (q >> 1) + (q & 1)
        by = by if back else (PW - by) % PW
        return pltpu.roll(a, by, 1) if by else a

    def rows_at(x, y, m, q):
        return f[(x + 1 - (q >> 1)) * CY + y + 1 - (q & 1), pl.ds(32 * m + 8 * q, 8), :]

    step = 0.5 / (speed[0:1, :] + 6.0)
    step_wide = 0.5 / (speed[0:1, 0:1] + 6.0)

    for j in range(NODES // 8):
        lat[pl.ds(j * 8, 8), :] = (
            nat[pl.ds(t0 + j * 8, 8), :] + step * nat[pl.ds(r0 + j * 8, 8), :]
        )

    put_t = pltpu.make_async_copy(lat, out_t, osem.at[0])
    put_t.start()
    for x in range(CX):
        total = sums[0, x] + step * sums[1, x]
        viscosity = ce[pl.ds(x * TR, 24), :] * jnp.exp(1.5 - 0.375 * total)
        vis[0, x] = viscosity
        vis[1, x] = 0.25 / viscosity

    forces = []
    for i in range(2):
        coefficient = ends[i, pl.ds(COEF, 1), :]
        temp, change = ends[i, pl.ds(TEMP, 1), :], ends[i, pl.ds(RATE, 1), :]
        viscosity = coefficient * jnp.exp(1.5 - 0.375 * (temp + step_wide * change))
        stabilize = 0.25 / viscosity
        forces.append(
            viscosity * fp[i, pl.ds(0, 32), :]
            + stabilize * fp[i, pl.ds(32, 32), :]
            + fp[i, pl.ds(64, 32), :]
        )
    last = sum(
        shifted(jnp.where(upper_wide, forces[1][8 * q : 8 * q + 8], forces[0][8 * q : 8 * q + 8]), q, True)
        for q in range(4)
    )
    zp[...] = last

    is_last = lane == LZ - 1

    def node_row(x, carry):
        ends_row = pltpu.roll(zp[...], PW - EY * (x + 1), 1)[:, :LZ]
        for y in range(LY):
            total = f2[x * LY + y]
            for q in range(4):
                cell_x, cell_y = x + 1 - (q >> 1), y + 1 - (q & 1)
                viscosity = vis[0, cell_x, pl.ds(7 + cell_y, 1), :]
                stabilize = vis[1, cell_x, pl.ds(7 + cell_y, 1), :]
                total = total + viscosity * rows_at(x, y, 0, q) + stabilize * rows_at(x, y, 1, q)
            total = jnp.where(is_last, pltpu.roll(ends_row, LZ - 2 - y, 1), total)
            nod[pl.ds(y * 8, 8), :] = total
        for h in range(2):
            at = pl.multiple_of(x * LY + 8 * h, 8)
            flags = mk[pl.ds(at, 8), :]
            for c in range(4):
                near = nod[pl.ds(64 * h + c, 8, stride=8), :]
                far = nod[pl.ds(64 * h + 4 + c, 8, stride=8), :]
                value = near + pltpu.roll(far, 1, 1)
                if c == 2:
                    value = value - 2.0 * lat[pl.ds(at, 8), :]
                state = nat[pl.ds(pl.multiple_of(c * NODES + at, 8), 8), :]
                res[c, pl.ds(at, 8), :] = jnp.where((flags & (1 << c)) != 0, state, value)
        return carry

    puts = [put_t]
    for h in range(2):
        lax.fori_loop(h * LX // 2, (h + 1) * LX // 2, node_row, 0)
        part = pl.ds(h * NODES // 2, NODES // 2)
        puts.append(pltpu.make_async_copy(res.at[:, part], out_r.at[:, part], osem.at[1 + h]))
        puts[-1].start()
    for put in puts:
        put.wait()


def solution(mesh):
    sizes = nx, ny, nz = tuple(mesh.shape[a] for a in ("gx", "gy", "gz"))
    vmem = pltpu.VMEM
    hbm_spec = pl.BlockSpec(memory_space=pltpu.HBM)
    vmem_spec = pl.BlockSpec(memory_space=vmem)

    def in_hbm(a):
        return pltpu.with_memory_space_constraint(a, pltpu.HBM)

    def shards(heat, rate, guess, rock, mask, rheo, ops):
        kept = pl.pallas_call(
            functools.partial(exchange, sizes),
            out_shape=(
                vmem((8 * NODES, LZ), F32),
                vmem((NODES, LZ), jnp.int32),
                vmem((CX * CY, 96, LZ), F32),
                vmem((NODES, 8, LZ), F32),
                vmem((2, 96, PW), F32),
                vmem((2, CX, 24, LZ), F32),
                vmem((EX * TR, LZ), F32),
                vmem((2, 8, PW), F32),
                vmem((8, LZ), F32),
            ),
            in_specs=[hbm_spec] * 7,
            out_specs=[vmem_spec] * 9,
            scratch_shapes=[
                pltpu.SMEM((4,), F32),
                vmem((3, 32, 32), F32),
                vmem((3 * NODES, LZ), F32),
                vmem((NODES, LZ), jnp.int32),
                vmem((EX * TR, LZ), F32),
                vmem((EX * TR, LZ), F32),
                vmem((2, 8 * LY, LZ), F32),
                vmem((2, 8 * LY, LZ), F32),
                vmem((2, 8 * LX, LZ), F32),
                vmem((2, 8 * LX, LZ), F32),
                vmem((4, 8, LZ), F32),
                vmem((4, 8, LZ), F32),
                vmem((2, LY, LZ), F32),
                vmem((2, LX, LZ), F32),
                vmem((2, 8, LZ), F32),
                vmem((2, 8, LZ), F32),
                vmem((2, 8, PW), F32),
                vmem((2, 8, PW), F32),
                vmem((3, max(nx * ny, 8), 1, LZ), F32),
                vmem((EX * EY, 16, LZ), BF16),
                vmem((96, 128), BF16),
                pltpu.SemaphoreType.DMA((7,)),
                pltpu.SemaphoreType.DMA((20,)),
                pltpu.SemaphoreType.DMA((20,)),
                pltpu.SemaphoreType.DMA((3,)),
                pltpu.SemaphoreType.DMA((3,)),
            ],
            compiler_params=pltpu.CompilerParams(
                collective_id=0, has_side_effects=True, vmem_limit_bytes=24 * 1024 * 1024
            ),
        )(
            in_hbm(rheo),
            in_hbm(ops),
            in_hbm(heat.reshape(NODES, LZ)),
            in_hbm(rate.reshape(3 * NODES, LZ)),
            in_hbm(guess.reshape(4 * NODES, LZ)),
            in_hbm(rock.reshape(NODES, LZ)),
            in_hbm(mask.reshape(NODES, LZ)),
        )
        out_t, out_r = pl.pallas_call(
            finish,
            out_shape=(pltpu.HBM((NODES, LZ), F32), pltpu.HBM((4, NODES, LZ), F32)),
            in_specs=[vmem_spec] * 9,
            out_specs=[hbm_spec] * 2,
            scratch_shapes=[
                vmem((2, CX, 24, LZ), F32),
                vmem((8 * LY, LZ), F32),
                vmem((8, PW), F32),
                vmem((NODES, LZ), F32),
                vmem((4, NODES, LZ), F32),
                pltpu.SemaphoreType.DMA((3,)),
            ],
            compiler_params=pltpu.CompilerParams(vmem_limit_bytes=24 * 1024 * 1024),
        )(*(pltpu.with_memory_space_constraint(a, vmem) for a in kept))
        return out_t.reshape(LX, LY, LZ), out_r.reshape(4, LX, LY, LZ)

    grid = P("gx", "gy", "gz")
    fields = P(None, "gx", "gy", "gz")
    return jax.shard_map(
        shards,
        mesh=mesh,
        in_specs=(grid, fields, fields, grid, grid, P(), P()),
        out_specs=(grid, fields),
        check_vma=False,
    )
```

```python
import functools

import jax
import jax.numpy as jnp
from jax import lax
from jax.experimental import pallas as pl
from jax.experimental.pallas import tpu as pltpu
from jax.sharding import PartitionSpec as P

MESH = pl.DeviceIdType.MESH
F32 = jnp.float32
BF16 = jnp.bfloat16

LX, LY, LZ = 8, 16, 128
NODES = LX * LY
EX, EY = LX + 2, LY + 2
CX, CY = LX + 1, LY + 1
TR = 32
PW = 256
COEF, TEMP, RATE = 4, 5, 6


def lanes(shape):
    return lax.broadcasted_iota(jnp.int32, shape, 1)


def exchange(
    sizes,
    rheo_in,
    ops_in,
    heat,
    rate,
    guess,
    rock,
    mask,
    nat,
    mk,
    f,
    f2,
    fp,
    sums,
    ce,
    ends,
    speed,
    rheo,
    ops,
    vel,
    rk,
    te,
    ge,
    sx,
    rx,
    sy,
    ry,
    se,
    re,
    rgx,
    rgy,
    stz,
    rtz,
    sp,
    rp,
    tops,
    xb,
    wts,
    lsem,
    ss,
    rs,
    ms,
    mr,
):
    nx, ny, nz = sizes
    gx, gy, gz = lax.axis_index("gx"), lax.axis_index("gy"), lax.axis_index("gz")
    has_x = (gx > 0, gx < nx - 1)
    has_y = (gy > 0, gy < ny - 1)
    has_z = (gz > 0, gz < nz - 1)

    locals_ = [
        pltpu.make_async_copy(rate, vel, lsem.at[0]),
        pltpu.make_async_copy(heat, nat.at[pl.ds(TEMP * NODES, NODES)], lsem.at[1]),
        pltpu.make_async_copy(guess, nat.at[pl.ds(0, 4 * NODES)], lsem.at[2]),
        pltpu.make_async_copy(rock, rk, lsem.at[3]),
        pltpu.make_async_copy(rheo_in, rheo, lsem.at[4]),
        pltpu.make_async_copy(ops_in, ops, lsem.at[5]),
        pltpu.make_async_copy(mask, mk, lsem.at[6]),
    ]
    for copy in locals_[:2]:
        copy.start()

    barrier = pltpu.get_barrier_semaphore()

    inner = min(nz, 8)
    gz_in, gz_out = lax.rem(gz, inner), gz // inner
    stages = (
        (nx * ny, gy * nx + gx, lambda t: {"gx": lax.rem(t, nx), "gy": t // nx}),
        (nz // inner, gz_out, lambda t: {"gz": t * inner + gz_in}),
        (inner, gz_in, lambda t: {"gz": gz_out * inner + t}),
    )
    step_x = ({"gx": gx - 1}, {"gx": gx + 1})
    step_y = ({"gy": gy - 1}, {"gy": gy + 1})
    step_z = ({"gz": gz - 1}, {"gz": gz + 1})
    step_e = [dict(**step_x[e // 2], **step_y[e % 2]) for e in range(4)]
    has_e = [jnp.logical_and(has_x[e // 2], has_y[e % 2]) for e in range(4)]

    def greet(device):
        pl.semaphore_signal(barrier, inc=1, device_id=device, device_id_type=MESH)

    def far_first(j, size):
        return 1 + lax.rem(j - 1 + size // 2, max(size - 1, 1))

    for size, own, at in stages:

        def greet_one(j, carry):
            greet(at(lax.rem(own + far_first(j, size), size)))
            return carry

        lax.fori_loop(1, size, greet_one, 0)

    greeted = sum(size - 1 for size, _, _ in stages)
    for d in range(2):

        @pl.when(has_z[d])
        def _():
            greet(step_z[d])

        greeted = greeted + has_z[d].astype(jnp.int32)

    for copy in locals_[2:]:
        copy.start()

    for d in range(2):

        @pl.when(jnp.logical_not(has_x[d]))
        def _():
            rx[d] = jnp.zeros((8 * LY, LZ), F32)
            rgx[d] = jnp.zeros((LY, LZ), F32)
            rx[d, pl.ds(COEF * LY, LY), :] = jnp.ones((LY, LZ), F32)

        @pl.when(jnp.logical_not(has_y[d]))
        def _():
            ry[d] = jnp.zeros((8 * LX, LZ), F32)
            rgy[d] = jnp.zeros((LX, LZ), F32)
            ry[d, pl.ds(COEF * LX, LX), :] = jnp.ones((LX, LZ), F32)

        @pl.when(jnp.logical_not(has_z[d]))
        def _():
            rtz[d] = jnp.zeros((8, LZ), F32)
            rp[d] = jnp.where(
                lax.broadcasted_iota(jnp.int32, (8, PW), 0) == COEF, 1.0, 0.0
            ).astype(F32)

    for e in range(4):

        @pl.when(jnp.logical_not(has_e[e]))
        def _():
            re[e] = jnp.where(
                lax.broadcasted_iota(jnp.int32, (8, LZ), 0) == COEF, 1.0, 0.0
            ).astype(F32)

    nat[pl.ds(7 * NODES, NODES), :] = jnp.zeros((NODES, LZ), F32)

    locals_[0].wait()
    top = jnp.abs(vel[pl.ds(0, 8), :])

    def top_step(i, top):
        for k in range(8):
            top = jnp.maximum(top, jnp.abs(vel[pl.ds(pl.multiple_of(i * 64 + k * 8, 8), 8), :]))
        return top

    top = lax.fori_loop(0, 3 * NODES // 64, top_step, top)
    tops[0, stages[0][1]] = jnp.max(top, axis=0, keepdims=True)

    locals_[1].wait()
    lane = lanes((8, LZ))
    t0 = TEMP * NODES
    for d in range(2):
        xs, ys = (0, LX - 1)[d], (0, LY - 1)[d]
        sx[d, pl.ds(TEMP * LY, LY), :] = nat[pl.ds(t0 + xs * LY, LY), :]
        sy[d, pl.ds(TEMP * LX, LX), :] = nat[pl.ds(t0 + ys, LX, stride=LY), :]
    low = jnp.zeros((8, LZ), F32)
    high = jnp.zeros((8, LZ), F32)
    for j in range(NODES // 8):
        r = nat[pl.ds(t0 + j * 8, 8), :]
        if j:
            r = pltpu.roll(r, j, 1)
        low = jnp.where(lane == j, r, low)
        high = jnp.where(lane == (j - 1) % LZ, r, high)
    stz[0] = low
    stz[1] = high

    locals_[2].wait()
    locals_[3].wait()
    locals_[4].wait()

    for i in range(NODES // 8):
        label = rk[pl.ds(i * 8, 8), :]
        total = jnp.zeros((8, LZ), F32)
        for k in range(4):
            total = total + jnp.where(label == k, rheo[k], 0.0)
        nat[pl.ds(COEF * NODES + i * 8, 8), :] = total
    for d in range(2):
        xs, ys = (0, LX - 1)[d], (0, LY - 1)[d]
        for k in range(5):
            sx[d, pl.ds(k * LY, LY), :] = nat[pl.ds(k * NODES + xs * LY, LY), :]
            sy[d, pl.ds(k * LX, LX), :] = nat[pl.ds(k * NODES + ys, LX, stride=LY), :]

    pl.semaphore_wait(barrier, greeted)

    def top_send(i):
        size, own, at = stages[i]

        def one(j, carry):
            pltpu.make_async_remote_copy(
                src_ref=tops.at[i, own],
                dst_ref=tops.at[i, own],
                send_sem=ms.at[i],
                recv_sem=mr.at[i],
                device_id=at(lax.rem(own + far_first(j, size), size)),
                device_id_type=MESH,
            ).start()
            return carry

        lax.fori_loop(1, size, one, 0)

    def top_wait(i, sem):
        if stages[i][0] > 1:
            rows = tops.at[i, pl.ds(0, stages[i][0] - 1)]
            pltpu.make_async_copy(rows, rows, sem.at[i]).wait()

    def top_gather(i):
        top_wait(i, mr)
        return jnp.max(tops[i, pl.ds(0, stages[i][0])], axis=0)

    def top_pass(i):
        tops[i + 1, stages[i + 1][1]] = top_gather(i)
        top_send(i + 1)


    def halo(src, dst, first, opposite, count, device, d, recv, rows=None, whole=False):
        slot = d if recv else opposite
        span = None if rows is None else rows[1 - d if recv else d]

        def part(ref, i, whole):
            return ref.at[i] if whole else ref.at[i, pl.ds(*span)]

        return pltpu.make_async_remote_copy(
            src_ref=part(src, d, rows is None),
            dst_ref=part(dst, slot, rows is None or whole),
            send_sem=ss.at[first + d],
            recv_sem=rs.at[first + slot],
            device_id=device,
            device_id_type=MESH,
        )

    def group(has, src, dst, first, devices, rows=None, whole=False):
        count = len(has)
        return [
            (
                has[d],
                functools.partial(halo, src, dst, first, count - 1 - d, count, devices[d], d, False, rows, whole),
                functools.partial(halo, src, dst, first, count - 1 - d, count, devices[d], d, True, rows, whole),
            )
            for d in range(count)
        ]

    temp_x = group(has_x, sx, rx, 0, step_x, ((TEMP * LY, LY),) * 2)
    temp_y = group(has_y, sy, ry, 2, step_y, ((TEMP * LX, LX),) * 2)
    temp_z = group(has_z, stz, rtz, 4, step_z)
    state_x = group(has_x, sx, rx, 6, step_x, ((0, 4 * LY), (0, 5 * LY)))
    state_y = group(has_y, sy, ry, 8, step_y, ((0, 4 * LX), (0, 5 * LX)))
    rate_x = group(has_x, sx, rgx, 10, step_x, ((RATE * LY, LY),) * 2, True)
    rate_y = group(has_y, sy, rgy, 12, step_y, ((RATE * LX, LX),) * 2, True)
    edges = group(has_e, se, re, 14, step_e)
    planes = group(has_z, sp, rp, 18, step_z)

    def start(copies):
        for has, send, _ in copies:

            @pl.when(has)
            def _():
                send().start()

    def wait(copies):
        for has, _, recv in copies:

            @pl.when(has)
            def _():
                recv().wait_recv()

    def sent(copies):
        for has, send, _ in copies:

            @pl.when(has)
            def _():
                send().wait_send()

    start(temp_y + temp_x + temp_z)
    top_send(0)
    start(state_y + state_x)

    row = lax.broadcasted_iota(jnp.int32, (32, 32), 0)
    col = lax.broadcasted_iota(jnp.int32, (32, 32), 1)
    from_row = 8 * (row & 3) + 2 * (row >> 3) + ((row >> 2) & 1)
    pick_row = jnp.where(col == from_row, 1.0, 0.0).astype(BF16)
    row = lax.broadcasted_iota(jnp.int32, (32, 128), 0)
    col = lax.broadcasted_iota(jnp.int32, (32, 128), 1)
    from_col = 8 * (col & 3) + 2 * ((col >> 4) & 3) + ((col >> 2) & 1)
    pick_col = jnp.where(row == from_col, 1.0, 0.0).astype(BF16)
    locals_[5].wait()
    for m in range(3):
        block = ops[m]
        head = block.astype(BF16)
        tail = (block - head.astype(F32)).astype(BF16)
        parts = []
        for part in (head, tail):
            part = jnp.dot(pick_row, part, preferred_element_type=F32).astype(BF16)
            parts.append(jnp.dot(part, pick_col, preferred_element_type=F32))
        wts[pl.ds(32 * m, 32), :] = jnp.where(col < 64, parts[0], parts[1]).astype(BF16)

    upper = lax.broadcasted_iota(jnp.int32, (8, LZ), 0) < 4

    def put_column(at, tile):
        both = jnp.where(upper, tile, pltpu.roll(pltpu.roll(tile, LZ - 1, 1), 4, 0))
        head = both.astype(BF16).astype(F32)
        xb[at] = jnp.concatenate([head, both - head], axis=0).astype(BF16)

    def own_columns(x, carry):
        for y in range(LY):
            put_column((x + 1) * EY + y + 1, nat[pl.ds(x * LY + y, 8, stride=NODES), :])
        return carry

    lax.fori_loop(0, LX, own_columns, 0)

    w = wts[...]

    def cell_matrix(x, y):
        a = xb[pl.ds(x * EY + y, 2)].reshape(32, LZ)
        b = xb[pl.ds((x + 1) * EY + y, 2)].reshape(32, LZ)
        return jnp.concatenate([a, b, a, b], axis=0)

    def middle(x, w):
        for y in range(1, LY, 2):
            pair = [cell_matrix(x, y)]
            if y + 1 < LY:
                pair.append(cell_matrix(x, y + 1))
            got = jnp.dot(w, jnp.concatenate(pair, axis=1), preferred_element_type=F32)
            for k in range(len(pair)):
                f[x * CY + y + k] = got[:, k * LZ : (k + 1) * LZ]

    def sides(x, present):
        pair = [
            jnp.where(jnp.logical_and(present, has_y[d]), cell_matrix(x, (0, LY)[d]), jnp.zeros((128, LZ), BF16))
            for d in range(2)
        ]
        got = jnp.dot(w, jnp.concatenate(pair, axis=1), preferred_element_type=F32)
        for k in range(2):
            f[x * CY + (0, LY)[k]] = got[:, k * LZ : (k + 1) * LZ]

    def inner_row(x, carry):
        middle(x, w)
        return carry

    lax.fori_loop(1, 3, inner_row, 0)

    wait(temp_y + temp_x + temp_z)

    def border(dst, field):
        for x in range(LX):
            dst[pl.ds((x + 1) * TR + 8, LY), :] = nat[pl.ds(field * NODES + x * LY, LY), :]

    def border_faces(dst, field, sides):
        for d in sides:
            dst[pl.ds((0, EX - 1)[d] * TR + 8, LY), :] = rx[d, pl.ds(field * LY, LY), :]
            dst[pl.ds(TR + (7, 8 + LY)[d], LX, stride=TR), :] = ry[d, pl.ds(field * LX, LX), :]

    def border_edges(dst, field, which):
        for e in which:
            at = (0, EX - 1)[e // 2] * TR + (7, 8 + LY)[e % 2]
            dst[pl.ds(at, 1), :] = re[e, pl.ds(field, 1), :]

    border(te, TEMP)
    border_faces(te, TEMP, (0, 1))
    for x in range(LX):
        for h in range(2):
            j = 2 * x + h
            at = (x + 1) * TR + 8 + 8 * h
            centre = te[pl.ds(at, 8), :]
            plus_x, minus_x = te[pl.ds(at + TR, 8), :], te[pl.ds(at - TR, 8), :]
            plus_y, minus_y = te[pl.ds(at + 1, 8), :], te[pl.ds(at - 1, 8), :]
            from_low = rtz[0] if j == 1 else pltpu.roll(rtz[0], (1 - j) % LZ, 1)
            from_high = pltpu.roll(rtz[1], LZ - 1 - j, 1)
            minus_z = jnp.where(lane == 0, from_low, pltpu.roll(centre, 1, 1))
            plus_z = jnp.where(lane == LZ - 1, from_high, pltpu.roll(centre, LZ - 1, 1))
            laplace = plus_x + minus_x + plus_y + minus_y + plus_z + minus_z - 6.0 * centre
            v = [vel[pl.ds(k * NODES + j * 8, 8), :] for k in range(3)]
            transport = (
                v[0] * (plus_x - minus_x) + v[1] * (plus_y - minus_y) + v[2] * (plus_z - minus_z)
            )
            nat[pl.ds(RATE * NODES + j * 8, 8), :] = laplace - 0.5 * transport
    r0 = RATE * NODES
    for d in range(2):
        xs, ys = (0, LX - 1)[d], (0, LY - 1)[d]
        sx[d, pl.ds(RATE * LY, LY), :] = nat[pl.ds(r0 + xs * LY, LY), :]
        sy[d, pl.ds(RATE * LX, LX), :] = nat[pl.ds(r0 + ys, LX, stride=LY), :]
    for e in range(4):
        at = (0, LX - 1)[e // 2] * LY + (0, LY - 1)[e % 2]
        se[e] = nat[pl.ds(at, 8, stride=NODES), :]
    start(rate_y + edges + rate_x)
    lax.fori_loop(3, 5, inner_row, 0)
    top_pass(0)
    lax.fori_loop(5, LX, inner_row, 0)

    def plane_row(tiles, first):
        low = jnp.zeros((8, LZ), F32)
        high = jnp.zeros((8, LZ), F32)
        for k, tile in enumerate(tiles):
            y = first + k
            r = pltpu.roll(tile, y, 1) if y else tile
            low = jnp.where(lane == y, r, low)
            high = jnp.where(lane == (y - 1) % LZ, r, high)
        return low, pltpu.roll(high, 1, 1)

    def add_plane(x, low, high):
        for i, part in enumerate((low, high)):
            wide = jnp.concatenate([part, jnp.zeros((8, PW - LZ), F32)], axis=1)
            sp[i] = sp[i] + pltpu.roll(wide, x * EY, 1)

    sp[...] = jnp.zeros((2, 8, PW), F32)

    def own_plane(x, carry):
        tiles = [nat[pl.ds(x * LY + y, 8, stride=NODES), :] for y in range(LY)]
        add_plane(x + 1, *plane_row(tiles, 1))
        return carry

    lax.fori_loop(0, LX, own_plane, 0)
    top_pass(1)

    ring = []
    for d in range(2):
        for y in range(LY):
            ring.append(
                ((0, EX - 1)[d], y + 1, functools.partial(lambda d, y: rx[d, pl.ds(y, 8, stride=LY), :], d, y))
            )
        for x in range(LX):
            ring.append(
                (x + 1, (0, EY - 1)[d], functools.partial(lambda d, x: ry[d, pl.ds(x, 8, stride=LX), :], d, x))
            )
    for e in range(4):
        ring.append(((0, EX - 1)[e // 2], (0, EY - 1)[e % 2], functools.partial(lambda e: re[e], e)))

    wait(state_y + state_x)
    for x, y, tile in ring[:-4]:
        put_column(x * EY + y, tile())
    for x in range(1, LX):
        sides(x, True)
    for d in range(2):
        middle((0, LX)[d], jnp.where(has_x[d], w, jnp.zeros((96, 128), BF16)))

    def rows_at(x, y, m, q):
        return f[(x + 1 - (q >> 1)) * CY + y + 1 - (q & 1), pl.ds(32 * m + 8 * q, 8), :]

    def fixed_row(x, carry):
        for y in range(LY):
            f2[x * LY + y] = sum(rows_at(x, y, 2, q) for q in range(4))
        return carry

    lax.fori_loop(1, LX - 1, fixed_row, 0)

    wait(rate_y + rate_x + edges)
    for d in range(2):
        rx[d, pl.ds(RATE * LY, LY), :] = rgx[d]
        ry[d, pl.ds(RATE * LX, LX), :] = rgy[d]
    halves = [[jnp.zeros((8, LZ), F32) for _ in range(PW // LZ)] for _ in range(2)]
    for x, y, tile in ring:
        at = x * EY + y
        r = tile()
        if at % LZ:
            r = pltpu.roll(r, at % LZ, 1)
        for i in range(2):
            to = (at - i) % PW
            halves[i][to // LZ] = jnp.where(lane == to % LZ, r, halves[i][to // LZ])
    sp[0] = sp[0] + jnp.concatenate(halves[0], axis=1)
    sp[1] = sp[1] + pltpu.roll(jnp.concatenate(halves[1], axis=1), 1, 1)
    start(planes)

    for x, y, tile in ring[-4:]:
        put_column(x * EY + y, tile())
    for d in range(2):
        sides((0, LX)[d], has_x[d])
    for x in (0, LX - 1):
        fixed_row(x, 0)

    border_edges(te, TEMP, range(4))
    border(ge, RATE)
    border_faces(ge, RATE, (0, 1))
    border_edges(ge, RATE, range(4))
    border(ce, COEF)
    border_faces(ce, COEF, (0,))
    border_edges(ce, COEF, (0,))

    for i, ref in enumerate((te, ge)):
        for x in range(CX):
            total = ref[pl.ds(x * TR, TR), :] + ref[pl.ds((x + 1) * TR, TR), :]
            total = total + pltpu.roll(total, LZ - 1, 1)
            total = total + pltpu.roll(total, TR - 1, 0)
            sums[i, x] = total[:24]

    top_wait(0, ms)
    top_wait(1, ms)
    sent(temp_x + temp_y + temp_z + state_x + state_y + rate_x + rate_y + edges)
    wait(planes)

    def shifted(a, q, back):
        by = EY * (q >> 1) + (q & 1)
        by = by if back else (PW - by) % PW
        return pltpu.roll(a, by, 1) if by else a

    place = lanes((8, PW))
    place_x = (place * 3641) >> 16
    place_y = place - EY * place_x
    outside = jnp.logical_or(
        jnp.logical_or(
            jnp.logical_and(place_x == 0, jnp.logical_not(has_x[0])),
            jnp.logical_and(place_x == LX, jnp.logical_not(has_x[1])),
        ),
        jnp.logical_or(
            jnp.logical_and(place_y == 0, jnp.logical_not(has_y[0])),
            jnp.logical_and(place_y == LY, jnp.logical_not(has_y[1])),
        ),
    )
    upper_wide = lax.broadcasted_iota(jnp.int32, (8, PW), 0) < 4
    for i in range(2):
        below, above = (rp[0], sp[0]) if i == 0 else (sp[1], rp[1])
        both = jnp.where(upper_wide, below, pltpu.roll(above, 4, 0))
        both = jnp.where(has_z[i], both, jnp.zeros((8, PW), F32))
        columns = []
        for q in range(4):
            part = jnp.where(outside, 0.0, shifted(both, q, False))
            head = part.astype(BF16).astype(F32)
            columns.append(jnp.concatenate([head, part - head], axis=0).astype(BF16))
        fp[i] = jnp.dot(w, jnp.concatenate(columns + columns, axis=0), preferred_element_type=F32)
        total = below + above
        total = sum(shifted(total, q, False) for q in range(4))
        ends[i] = total
        ends[i, pl.ds(COEF, 1), :] = below[COEF : COEF + 1]

    speed[...] = jnp.broadcast_to(jnp.max(top_gather(2), axis=1, keepdims=True), (8, LZ))
    locals_[6].wait()

    top_wait(2, ms)
    sent(planes)


def finish(
    nat,
    mk,
    f,
    f2,
    fp,
    sums,
    ce,
    ends,
    speed,
    out_t,
    out_r,
    vis,
    nod,
    zp,
    lat,
    res,
    osem,
):
    t0, r0 = TEMP * NODES, RATE * NODES
    lane = lanes((8, LZ))
    upper_wide = lax.broadcasted_iota(jnp.int32, (8, PW), 0) < 4

    def shifted(a, q, back):
        by = EY * (q >> 1) + (q & 1)
        by = by if back else (PW - by) % PW
        return pltpu.roll(a, by, 1) if by else a

    def rows_at(x, y, m, q):
        return f[(x + 1 - (q >> 1)) * CY + y + 1 - (q & 1), pl.ds(32 * m + 8 * q, 8), :]

    step = 0.5 / (speed[0:1, :] + 6.0)
    step_wide = 0.5 / (speed[0:1, 0:1] + 6.0)

    for j in range(NODES // 8):
        lat[pl.ds(j * 8, 8), :] = (
            nat[pl.ds(t0 + j * 8, 8), :] + step * nat[pl.ds(r0 + j * 8, 8), :]
        )

    put_t = pltpu.make_async_copy(lat, out_t, osem.at[0])
    put_t.start()
    for x in range(CX):
        total = sums[0, x] + step * sums[1, x]
        viscosity = ce[pl.ds(x * TR, 24), :] * jnp.exp(1.5 - 0.375 * total)
        vis[0, x] = viscosity
        vis[1, x] = 0.25 / viscosity

    forces = []
    for i in range(2):
        coefficient = ends[i, pl.ds(COEF, 1), :]
        temp, change = ends[i, pl.ds(TEMP, 1), :], ends[i, pl.ds(RATE, 1), :]
        viscosity = coefficient * jnp.exp(1.5 - 0.375 * (temp + step_wide * change))
        stabilize = 0.25 / viscosity
        forces.append(
            viscosity * fp[i, pl.ds(0, 32), :]
            + stabilize * fp[i, pl.ds(32, 32), :]
            + fp[i, pl.ds(64, 32), :]
        )
    last = sum(
        shifted(jnp.where(upper_wide, forces[1][8 * q : 8 * q + 8], forces[0][8 * q : 8 * q + 8]), q, True)
        for q in range(4)
    )
    zp[...] = last

    is_last = lane == LZ - 1

    def node_row(x, carry):
        ends_row = pltpu.roll(zp[...], PW - EY * (x + 1), 1)[:, :LZ]
        for y in range(LY):
            total = f2[x * LY + y]
            for q in range(4):
                cell_x, cell_y = x + 1 - (q >> 1), y + 1 - (q & 1)
                viscosity = vis[0, cell_x, pl.ds(7 + cell_y, 1), :]
                stabilize = vis[1, cell_x, pl.ds(7 + cell_y, 1), :]
                total = total + viscosity * rows_at(x, y, 0, q) + stabilize * rows_at(x, y, 1, q)
            total = jnp.where(is_last, pltpu.roll(ends_row, LZ - 2 - y, 1), total)
            nod[pl.ds(y * 8, 8), :] = total
        for h in range(2):
            at = pl.multiple_of(x * LY + 8 * h, 8)
            flags = mk[pl.ds(at, 8), :]
            for c in range(4):
                near = nod[pl.ds(64 * h + c, 8, stride=8), :]
                far = nod[pl.ds(64 * h + 4 + c, 8, stride=8), :]
                value = near + pltpu.roll(far, 1, 1)
                if c == 2:
                    value = value - 2.0 * lat[pl.ds(at, 8), :]
                state = nat[pl.ds(pl.multiple_of(c * NODES + at, 8), 8), :]
                res[c, pl.ds(at, 8), :] = jnp.where((flags & (1 << c)) != 0, state, value)
        return carry

    puts = [put_t]
    for h in range(4):
        lax.fori_loop(h * LX // 4, (h + 1) * LX // 4, node_row, 0)
        part = pl.ds(h * NODES // 4, NODES // 4)
        puts.append(pltpu.make_async_copy(res.at[:, part], out_r.at[:, part], osem.at[1 + h]))
        puts[-1].start()
    for put in puts:
        put.wait()


def solution(mesh):
    sizes = nx, ny, nz = tuple(mesh.shape[a] for a in ("gx", "gy", "gz"))
    vmem = pltpu.VMEM
    hbm_spec = pl.BlockSpec(memory_space=pltpu.HBM)
    vmem_spec = pl.BlockSpec(memory_space=vmem)

    def in_hbm(a):
        return pltpu.with_memory_space_constraint(a, pltpu.HBM)

    def shards(heat, rate, guess, rock, mask, rheo, ops):
        kept = pl.pallas_call(
            functools.partial(exchange, sizes),
            out_shape=(
                vmem((8 * NODES, LZ), F32),
                vmem((NODES, LZ), jnp.int32),
                vmem((CX * CY, 96, LZ), F32),
                vmem((NODES, 8, LZ), F32),
                vmem((2, 96, PW), F32),
                vmem((2, CX, 24, LZ), F32),
                vmem((EX * TR, LZ), F32),
                vmem((2, 8, PW), F32),
                vmem((8, LZ), F32),
            ),
            in_specs=[hbm_spec] * 7,
            out_specs=[vmem_spec] * 9,
            scratch_shapes=[
                pltpu.SMEM((4,), F32),
                vmem((3, 32, 32), F32),
                vmem((3 * NODES, LZ), F32),
                vmem((NODES, LZ), jnp.int32),
                vmem((EX * TR, LZ), F32),
                vmem((EX * TR, LZ), F32),
                vmem((2, 8 * LY, LZ), F32),
                vmem((2, 8 * LY, LZ), F32),
                vmem((2, 8 * LX, LZ), F32),
                vmem((2, 8 * LX, LZ), F32),
                vmem((4, 8, LZ), F32),
                vmem((4, 8, LZ), F32),
                vmem((2, LY, LZ), F32),
                vmem((2, LX, LZ), F32),
                vmem((2, 8, LZ), F32),
                vmem((2, 8, LZ), F32),
                vmem((2, 8, PW), F32),
                vmem((2, 8, PW), F32),
                vmem((3, max(nx * ny, 8), 1, LZ), F32),
                vmem((EX * EY, 16, LZ), BF16),
                vmem((96, 128), BF16),
                pltpu.SemaphoreType.DMA((7,)),
                pltpu.SemaphoreType.DMA((20,)),
                pltpu.SemaphoreType.DMA((20,)),
                pltpu.SemaphoreType.DMA((3,)),
                pltpu.SemaphoreType.DMA((3,)),
            ],
            compiler_params=pltpu.CompilerParams(
                collective_id=0, has_side_effects=True, vmem_limit_bytes=24 * 1024 * 1024
            ),
        )(
            in_hbm(rheo),
            in_hbm(ops),
            in_hbm(heat.reshape(NODES, LZ)),
            in_hbm(rate.reshape(3 * NODES, LZ)),
            in_hbm(guess.reshape(4 * NODES, LZ)),
            in_hbm(rock.reshape(NODES, LZ)),
            in_hbm(mask.reshape(NODES, LZ)),
        )
        out_t, out_r = pl.pallas_call(
            finish,
            out_shape=(pltpu.HBM((NODES, LZ), F32), pltpu.HBM((4, NODES, LZ), F32)),
            in_specs=[vmem_spec] * 9,
            out_specs=[hbm_spec] * 2,
            scratch_shapes=[
                vmem((2, CX, 24, LZ), F32),
                vmem((8 * LY, LZ), F32),
                vmem((8, PW), F32),
                vmem((NODES, LZ), F32),
                vmem((4, NODES, LZ), F32),
                pltpu.SemaphoreType.DMA((5,)),
            ],
            compiler_params=pltpu.CompilerParams(vmem_limit_bytes=24 * 1024 * 1024),
        )(*(pltpu.with_memory_space_constraint(a, vmem) for a in kept))
        return out_t.reshape(LX, LY, LZ), out_r.reshape(4, LX, LY, LZ)

    grid = P("gx", "gy", "gz")
    fields = P(None, "gx", "gy", "gz")
    return jax.shard_map(
        shards,
        mesh=mesh,
        in_specs=(grid, fields, fields, grid, grid, P(), P()),
        out_specs=(grid, fields),
        check_vma=False,
    )
```

```python
import functools

import jax
import jax.numpy as jnp
from jax import lax
from jax.experimental import pallas as pl
from jax.experimental.pallas import tpu as pltpu
from jax.sharding import PartitionSpec as P

MESH = pl.DeviceIdType.MESH
F32 = jnp.float32
BF16 = jnp.bfloat16

LX, LY, LZ = 8, 16, 128
NODES = LX * LY
EX, EY = LX + 2, LY + 2
CX, CY = LX + 1, LY + 1
TR = 32
PW = 256
COEF, TEMP, RATE = 4, 5, 6


def lanes(shape):
    return lax.broadcasted_iota(jnp.int32, shape, 1)


def exchange(
    sizes,
    rheo_in,
    ops_in,
    heat,
    rate,
    guess,
    rock,
    mask,
    nat,
    mk,
    f,
    f2,
    fp,
    sums,
    ce,
    ends,
    speed,
    rheo,
    ops,
    vel,
    rk,
    te,
    ge,
    sx,
    rx,
    sy,
    ry,
    se,
    re,
    stz,
    rtz,
    sp,
    rp,
    tops,
    xb,
    wts,
    lsem,
    ss,
    rs,
    ms,
    mr,
):
    nx, ny, nz = sizes
    gx, gy, gz = lax.axis_index("gx"), lax.axis_index("gy"), lax.axis_index("gz")
    has_x = (gx > 0, gx < nx - 1)
    has_y = (gy > 0, gy < ny - 1)
    has_z = (gz > 0, gz < nz - 1)

    locals_ = [
        pltpu.make_async_copy(rate, vel, lsem.at[0]),
        pltpu.make_async_copy(heat, nat.at[pl.ds(TEMP * NODES, NODES)], lsem.at[1]),
        pltpu.make_async_copy(guess, nat.at[pl.ds(0, 4 * NODES)], lsem.at[2]),
        pltpu.make_async_copy(rock, rk, lsem.at[3]),
        pltpu.make_async_copy(rheo_in, rheo, lsem.at[4]),
        pltpu.make_async_copy(ops_in, ops, lsem.at[5]),
        pltpu.make_async_copy(mask, mk, lsem.at[6]),
    ]
    for copy in locals_[:2]:
        copy.start()

    barrier = pltpu.get_barrier_semaphore()

    stages = (
        (nx * ny, gy * nx + gx, lambda t: {"gx": lax.rem(t, nx), "gy": t // nx}),
        (nz, gz, lambda t: {"gz": t}),
    )
    step_x = ({"gx": gx - 1}, {"gx": gx + 1})
    step_y = ({"gy": gy - 1}, {"gy": gy + 1})
    step_z = ({"gz": gz - 1}, {"gz": gz + 1})
    step_e = [dict(**step_x[e // 2], **step_y[e % 2]) for e in range(4)]
    has_e = [jnp.logical_and(has_x[e // 2], has_y[e % 2]) for e in range(4)]

    def greet(device):
        pl.semaphore_signal(barrier, inc=1, device_id=device, device_id_type=MESH)

    def far_first(j, size):
        return 1 + lax.rem(j - 1 + size // 2, max(size - 1, 1))

    for size, own, at in stages:

        def greet_one(j, carry):
            greet(at(lax.rem(own + far_first(j, size), size)))
            return carry

        lax.fori_loop(1, size, greet_one, 0)

    for copy in locals_[2:]:
        copy.start()

    for d in range(2):

        @pl.when(jnp.logical_not(has_x[d]))
        def _():
            rx[d] = jnp.zeros((8 * LY, LZ), F32)
            rx[d, pl.ds(COEF * LY, LY), :] = jnp.ones((LY, LZ), F32)

        @pl.when(jnp.logical_not(has_y[d]))
        def _():
            ry[d] = jnp.zeros((8 * LX, LZ), F32)
            ry[d, pl.ds(COEF * LX, LX), :] = jnp.ones((LX, LZ), F32)

        @pl.when(jnp.logical_not(has_z[d]))
        def _():
            rtz[d] = jnp.zeros((8, LZ), F32)
            rp[d] = jnp.where(
                lax.broadcasted_iota(jnp.int32, (8, PW), 0) == COEF, 1.0, 0.0
            ).astype(F32)

    for e in range(4):

        @pl.when(jnp.logical_not(has_e[e]))
        def _():
            re[e] = jnp.where(
                lax.broadcasted_iota(jnp.int32, (8, LZ), 0) == COEF, 1.0, 0.0
            ).astype(F32)

    nat[pl.ds(7 * NODES, NODES), :] = jnp.zeros((NODES, LZ), F32)

    locals_[0].wait()
    top = jnp.abs(vel[pl.ds(0, 8), :])

    def top_step(i, top):
        for k in range(8):
            top = jnp.maximum(top, jnp.abs(vel[pl.ds(pl.multiple_of(i * 64 + k * 8, 8), 8), :]))
        return top

    top = lax.fori_loop(0, 3 * NODES // 64, top_step, top)
    tops[0, stages[0][1]] = jnp.max(top, axis=0, keepdims=True)

    locals_[1].wait()
    lane = lanes((8, LZ))
    t0 = TEMP * NODES
    for d in range(2):
        xs, ys = (0, LX - 1)[d], (0, LY - 1)[d]
        sx[d, pl.ds(TEMP * LY, LY), :] = nat[pl.ds(t0 + xs * LY, LY), :]
        sy[d, pl.ds(TEMP * LX, LX), :] = nat[pl.ds(t0 + ys, LX, stride=LY), :]
    low = jnp.zeros((8, LZ), F32)
    high = jnp.zeros((8, LZ), F32)
    for j in range(NODES // 8):
        r = nat[pl.ds(t0 + j * 8, 8), :]
        if j:
            r = pltpu.roll(r, j, 1)
        low = jnp.where(lane == j, r, low)
        high = jnp.where(lane == (j - 1) % LZ, r, high)
    stz[0] = low
    stz[1] = high

    locals_[2].wait()
    locals_[3].wait()
    locals_[4].wait()

    for i in range(NODES // 8):
        label = rk[pl.ds(i * 8, 8), :]
        total = jnp.zeros((8, LZ), F32)
        for k in range(4):
            total = total + jnp.where(label == k, rheo[k], 0.0)
        nat[pl.ds(COEF * NODES + i * 8, 8), :] = total
    for d in range(2):
        xs, ys = (0, LX - 1)[d], (0, LY - 1)[d]
        for k in range(5):
            sx[d, pl.ds(k * LY, LY), :] = nat[pl.ds(k * NODES + xs * LY, LY), :]
            sy[d, pl.ds(k * LX, LX), :] = nat[pl.ds(k * NODES + ys, LX, stride=LY), :]
    pl.semaphore_wait(barrier, nx * ny - 1 + nz - 1)

    def top_send(i):
        size, own, at = stages[i]

        def one(j, carry):
            pltpu.make_async_remote_copy(
                src_ref=tops.at[i, own],
                dst_ref=tops.at[i, own],
                send_sem=ms.at[i],
                recv_sem=mr.at[i],
                device_id=at(lax.rem(own + far_first(j, size), size)),
                device_id_type=MESH,
            ).start()
            return carry

        lax.fori_loop(1, size, one, 0)

    def top_wait(i, sem):
        rows = tops.at[i, pl.ds(0, stages[i][0] - 1)]
        pltpu.make_async_copy(rows, rows, sem.at[i]).wait()

    def top_gather(i):
        top_wait(i, mr)
        return jnp.max(tops[i, pl.ds(0, stages[i][0])], axis=0)

    def top_pass(i):
        tops[i + 1, stages[i + 1][1]] = top_gather(i)
        top_send(i + 1)


    def halo(src, dst, first, opposite, count, device, d, recv, rows=None):
        slot = d if recv else opposite
        span = None if rows is None else rows[1 - d if recv else d]
        part = (lambda ref, i: ref.at[i]) if rows is None else (lambda ref, i: ref.at[i, pl.ds(*span)])
        return pltpu.make_async_remote_copy(
            src_ref=part(src, d),
            dst_ref=part(dst, slot),
            send_sem=ss.at[first + d],
            recv_sem=rs.at[first + slot],
            device_id=device,
            device_id_type=MESH,
        )

    def group(has, src, dst, first, devices, rows=None):
        count = len(has)
        return [
            (
                has[d],
                functools.partial(halo, src, dst, first, count - 1 - d, count, devices[d], d, False, rows),
                functools.partial(halo, src, dst, first, count - 1 - d, count, devices[d], d, True, rows),
            )
            for d in range(count)
        ]

    temp_x = group(has_x, sx, rx, 0, step_x, ((TEMP * LY, LY),) * 2)
    temp_y = group(has_y, sy, ry, 2, step_y, ((TEMP * LX, LX),) * 2)
    temp_z = group(has_z, stz, rtz, 4, step_z)
    state_x = group(has_x, sx, rx, 6, step_x, ((0, 4 * LY), (0, 5 * LY)))
    state_y = group(has_y, sy, ry, 8, step_y, ((0, 4 * LX), (0, 5 * LX)))
    rate_x = group(has_x, sx, rx, 10, step_x, ((RATE * LY, LY),) * 2)
    rate_y = group(has_y, sy, ry, 12, step_y, ((RATE * LX, LX),) * 2)
    edges = group(has_e, se, re, 14, step_e)
    planes = group(has_z, sp, rp, 18, step_z)

    def start(copies):
        for has, send, _ in copies:

            @pl.when(has)
            def _():
                send().start()

    def wait(copies):
        for has, _, recv in copies:

            @pl.when(has)
            def _():
                recv().wait_recv()

    def sent(copies):
        for has, send, _ in copies:

            @pl.when(has)
            def _():
                send().wait_send()

    start(temp_y + temp_x + temp_z)
    top_send(0)

    start(state_y + state_x)

    row = lax.broadcasted_iota(jnp.int32, (32, 32), 0)
    col = lax.broadcasted_iota(jnp.int32, (32, 32), 1)
    from_row = 8 * (row & 3) + 2 * (row >> 3) + ((row >> 2) & 1)
    pick_row = jnp.where(col == from_row, 1.0, 0.0).astype(BF16)
    row = lax.broadcasted_iota(jnp.int32, (32, 128), 0)
    col = lax.broadcasted_iota(jnp.int32, (32, 128), 1)
    from_col = 8 * (col & 3) + 2 * ((col >> 4) & 3) + ((col >> 2) & 1)
    pick_col = jnp.where(row == from_col, 1.0, 0.0).astype(BF16)
    locals_[5].wait()
    for m in range(3):
        block = ops[m]
        head = block.astype(BF16)
        tail = (block - head.astype(F32)).astype(BF16)
        parts = []
        for part in (head, tail):
            part = jnp.dot(pick_row, part, preferred_element_type=F32).astype(BF16)
            parts.append(jnp.dot(part, pick_col, preferred_element_type=F32))
        wts[pl.ds(32 * m, 32), :] = jnp.where(col < 64, parts[0], parts[1]).astype(BF16)

    upper = lax.broadcasted_iota(jnp.int32, (8, LZ), 0) < 4

    def put_column(at, tile):
        both = jnp.where(upper, tile, pltpu.roll(pltpu.roll(tile, LZ - 1, 1), 4, 0))
        head = both.astype(BF16).astype(F32)
        xb[at] = jnp.concatenate([head, both - head], axis=0).astype(BF16)

    def own_columns(x, carry):
        for y in range(LY):
            put_column((x + 1) * EY + y + 1, nat[pl.ds(x * LY + y, 8, stride=NODES), :])
        return carry

    lax.fori_loop(0, LX, own_columns, 0)

    w = wts[...]

    def cell_matrix(x, y):
        a = xb[pl.ds(x * EY + y, 2)].reshape(32, LZ)
        b = xb[pl.ds((x + 1) * EY + y, 2)].reshape(32, LZ)
        return jnp.concatenate([a, b, a, b], axis=0)

    def middle(x, w):
        for y in range(1, LY, 2):
            pair = [cell_matrix(x, y)]
            if y + 1 < LY:
                pair.append(cell_matrix(x, y + 1))
            got = jnp.dot(w, jnp.concatenate(pair, axis=1), preferred_element_type=F32)
            for k in range(len(pair)):
                f[x * CY + y + k] = got[:, k * LZ : (k + 1) * LZ]

    def sides(x, present):
        pair = [
            jnp.where(jnp.logical_and(present, has_y[d]), cell_matrix(x, (0, LY)[d]), jnp.zeros((128, LZ), BF16))
            for d in range(2)
        ]
        got = jnp.dot(w, jnp.concatenate(pair, axis=1), preferred_element_type=F32)
        for k in range(2):
            f[x * CY + (0, LY)[k]] = got[:, k * LZ : (k + 1) * LZ]

    def inner_row(x, carry):
        middle(x, w)
        return carry

    lax.fori_loop(1, 3, inner_row, 0)

    wait(temp_y + temp_x + temp_z)

    def border(dst, field):
        for x in range(LX):
            dst[pl.ds((x + 1) * TR + 8, LY), :] = nat[pl.ds(field * NODES + x * LY, LY), :]

    def border_faces(dst, field, sides):
        for d in sides:
            dst[pl.ds((0, EX - 1)[d] * TR + 8, LY), :] = rx[d, pl.ds(field * LY, LY), :]
            dst[pl.ds(TR + (7, 8 + LY)[d], LX, stride=TR), :] = ry[d, pl.ds(field * LX, LX), :]

    def border_edges(dst, field, which):
        for e in which:
            at = (0, EX - 1)[e // 2] * TR + (7, 8 + LY)[e % 2]
            dst[pl.ds(at, 1), :] = re[e, pl.ds(field, 1), :]

    border(te, TEMP)
    border_faces(te, TEMP, (0, 1))
    for x in range(LX):
        for h in range(2):
            j = 2 * x + h
            at = (x + 1) * TR + 8 + 8 * h
            centre = te[pl.ds(at, 8), :]
            plus_x, minus_x = te[pl.ds(at + TR, 8), :], te[pl.ds(at - TR, 8), :]
            plus_y, minus_y = te[pl.ds(at + 1, 8), :], te[pl.ds(at - 1, 8), :]
            from_low = rtz[0] if j == 1 else pltpu.roll(rtz[0], (1 - j) % LZ, 1)
            from_high = pltpu.roll(rtz[1], LZ - 1 - j, 1)
            minus_z = jnp.where(lane == 0, from_low, pltpu.roll(centre, 1, 1))
            plus_z = jnp.where(lane == LZ - 1, from_high, pltpu.roll(centre, LZ - 1, 1))
            laplace = plus_x + minus_x + plus_y + minus_y + plus_z + minus_z - 6.0 * centre
            v = [vel[pl.ds(k * NODES + j * 8, 8), :] for k in range(3)]
            transport = (
                v[0] * (plus_x - minus_x) + v[1] * (plus_y - minus_y) + v[2] * (plus_z - minus_z)
            )
            nat[pl.ds(RATE * NODES + j * 8, 8), :] = laplace - 0.5 * transport
    r0 = RATE * NODES
    for d in range(2):
        xs, ys = (0, LX - 1)[d], (0, LY - 1)[d]
        sx[d, pl.ds(RATE * LY, LY), :] = nat[pl.ds(r0 + xs * LY, LY), :]
        sy[d, pl.ds(RATE * LX, LX), :] = nat[pl.ds(r0 + ys, LX, stride=LY), :]
    for e in range(4):
        at = (0, LX - 1)[e // 2] * LY + (0, LY - 1)[e % 2]
        se[e] = nat[pl.ds(at, 8, stride=NODES), :]
    start(rate_y + edges + rate_x)
    lax.fori_loop(3, LX, inner_row, 0)
    top_pass(0)

    def plane_row(tiles, first):
        low = jnp.zeros((8, LZ), F32)
        high = jnp.zeros((8, LZ), F32)
        for k, tile in enumerate(tiles):
            y = first + k
            r = pltpu.roll(tile, y, 1) if y else tile
            low = jnp.where(lane == y, r, low)
            high = jnp.where(lane == (y - 1) % LZ, r, high)
        return low, pltpu.roll(high, 1, 1)

    def add_plane(x, low, high):
        for i, part in enumerate((low, high)):
            wide = jnp.concatenate([part, jnp.zeros((8, PW - LZ), F32)], axis=1)
            sp[i] = sp[i] + pltpu.roll(wide, x * EY, 1)

    sp[...] = jnp.zeros((2, 8, PW), F32)

    def own_plane(x, carry):
        tiles = [nat[pl.ds(x * LY + y, 8, stride=NODES), :] for y in range(LY)]
        add_plane(x + 1, *plane_row(tiles, 1))
        return carry

    lax.fori_loop(0, LX, own_plane, 0)

    wait(state_y + state_x + rate_y + rate_x + edges)
    ring = []
    for d in range(2):
        x = (0, EX - 1)[d]
        ring.append((x, 0, functools.partial(lambda e: re[e], 2 * d)))
        for y in range(LY):
            ring.append((x, y + 1, functools.partial(lambda d, y: rx[d, pl.ds(y, 8, stride=LY), :], d, y)))
        ring.append((x, EY - 1, functools.partial(lambda e: re[e], 2 * d + 1)))
    for x in range(LX):
        for d in range(2):
            ring.append(
                (x + 1, (0, EY - 1)[d], functools.partial(lambda d, x: ry[d, pl.ds(x, 8, stride=LX), :], d, x))
            )
    halves = [[jnp.zeros((8, LZ), F32) for _ in range(PW // LZ)] for _ in range(2)]
    for x, y, tile in ring:
        at = x * EY + y
        r = tile()
        if at % LZ:
            r = pltpu.roll(r, at % LZ, 1)
        for i in range(2):
            to = (at - i) % PW
            halves[i][to // LZ] = jnp.where(lane == to % LZ, r, halves[i][to // LZ])
    sp[0] = sp[0] + jnp.concatenate(halves[0], axis=1)
    sp[1] = sp[1] + pltpu.roll(jnp.concatenate(halves[1], axis=1), 1, 1)
    start(planes)

    for x, y, tile in ring:
        put_column(x * EY + y, tile())

    for x in range(1, LX):
        sides(x, True)
    for d in range(2):
        x = (0, LX)[d]
        middle(x, jnp.where(has_x[d], w, jnp.zeros((96, 128), BF16)))
        sides(x, has_x[d])

    def rows_at(x, y, m, q):
        return f[(x + 1 - (q >> 1)) * CY + y + 1 - (q & 1), pl.ds(32 * m + 8 * q, 8), :]

    def fixed_row(x, carry):
        for y in range(LY):
            f2[x * LY + y] = sum(rows_at(x, y, 2, q) for q in range(4))
        return carry

    lax.fori_loop(0, LX, fixed_row, 0)

    border_edges(te, TEMP, range(4))
    border(ge, RATE)
    border_faces(ge, RATE, (0, 1))
    border_edges(ge, RATE, range(4))
    border(ce, COEF)
    border_faces(ce, COEF, (0,))
    border_edges(ce, COEF, (0,))

    for i, ref in enumerate((te, ge)):
        for x in range(CX):
            total = ref[pl.ds(x * TR, TR), :] + ref[pl.ds((x + 1) * TR, TR), :]
            total = total + pltpu.roll(total, LZ - 1, 1)
            total = total + pltpu.roll(total, TR - 1, 0)
            sums[i, x] = total[:24]

    top_wait(0, ms)
    sent(temp_x + temp_y + temp_z + state_x + state_y + rate_x + rate_y + edges)
    wait(planes)

    def shifted(a, q, back):
        by = EY * (q >> 1) + (q & 1)
        by = by if back else (PW - by) % PW
        return pltpu.roll(a, by, 1) if by else a

    place = lanes((8, PW))
    place_x = (place * 3641) >> 16
    place_y = place - EY * place_x
    outside = jnp.logical_or(
        jnp.logical_or(
            jnp.logical_and(place_x == 0, jnp.logical_not(has_x[0])),
            jnp.logical_and(place_x == LX, jnp.logical_not(has_x[1])),
        ),
        jnp.logical_or(
            jnp.logical_and(place_y == 0, jnp.logical_not(has_y[0])),
            jnp.logical_and(place_y == LY, jnp.logical_not(has_y[1])),
        ),
    )
    upper_wide = lax.broadcasted_iota(jnp.int32, (8, PW), 0) < 4
    for i in range(2):
        below, above = (rp[0], sp[0]) if i == 0 else (sp[1], rp[1])
        both = jnp.where(upper_wide, below, pltpu.roll(above, 4, 0))
        both = jnp.where(has_z[i], both, jnp.zeros((8, PW), F32))
        columns = []
        for q in range(4):
            part = jnp.where(outside, 0.0, shifted(both, q, False))
            head = part.astype(BF16).astype(F32)
            columns.append(jnp.concatenate([head, part - head], axis=0).astype(BF16))
        fp[i] = jnp.dot(w, jnp.concatenate(columns + columns, axis=0), preferred_element_type=F32)
        total = below + above
        total = sum(shifted(total, q, False) for q in range(4))
        ends[i] = total
        ends[i, pl.ds(COEF, 1), :] = below[COEF : COEF + 1]

    speed[...] = jnp.broadcast_to(jnp.max(top_gather(1), axis=1, keepdims=True), (8, LZ))
    locals_[6].wait()

    top_wait(1, ms)
    sent(planes)


def finish(
    nat,
    mk,
    f,
    f2,
    fp,
    sums,
    ce,
    ends,
    speed,
    out_t,
    out_r,
    vis,
    nod,
    zp,
    lat,
    res,
    osem,
):
    t0, r0 = TEMP * NODES, RATE * NODES
    lane = lanes((8, LZ))
    upper_wide = lax.broadcasted_iota(jnp.int32, (8, PW), 0) < 4

    def shifted(a, q, back):
        by = EY * (q >> 1) + (q & 1)
        by = by if back else (PW - by) % PW
        return pltpu.roll(a, by, 1) if by else a

    def rows_at(x, y, m, q):
        return f[(x + 1 - (q >> 1)) * CY + y + 1 - (q & 1), pl.ds(32 * m + 8 * q, 8), :]

    step = 0.5 / (speed[0:1, :] + 6.0)
    step_wide = 0.5 / (speed[0:1, 0:1] + 6.0)

    for j in range(NODES // 8):
        lat[pl.ds(j * 8, 8), :] = (
            nat[pl.ds(t0 + j * 8, 8), :] + step * nat[pl.ds(r0 + j * 8, 8), :]
        )

    put_t = pltpu.make_async_copy(lat, out_t, osem.at[0])
    put_t.start()
    for x in range(CX):
        total = sums[0, x] + step * sums[1, x]
        viscosity = ce[pl.ds(x * TR, 24), :] * jnp.exp(1.5 - 0.375 * total)
        vis[0, x] = viscosity
        vis[1, x] = 0.25 / viscosity

    forces = []
    for i in range(2):
        coefficient = ends[i, pl.ds(COEF, 1), :]
        temp, change = ends[i, pl.ds(TEMP, 1), :], ends[i, pl.ds(RATE, 1), :]
        viscosity = coefficient * jnp.exp(1.5 - 0.375 * (temp + step_wide * change))
        stabilize = 0.25 / viscosity
        forces.append(
            viscosity * fp[i, pl.ds(0, 32), :]
            + stabilize * fp[i, pl.ds(32, 32), :]
            + fp[i, pl.ds(64, 32), :]
        )
    last = sum(
        shifted(jnp.where(upper_wide, forces[1][8 * q : 8 * q + 8], forces[0][8 * q : 8 * q + 8]), q, True)
        for q in range(4)
    )
    zp[...] = last

    is_last = lane == LZ - 1

    def node_row(x, carry):
        ends_row = pltpu.roll(zp[...], PW - EY * (x + 1), 1)[:, :LZ]
        for y in range(LY):
            total = f2[x * LY + y]
            for q in range(4):
                cell_x, cell_y = x + 1 - (q >> 1), y + 1 - (q & 1)
                viscosity = vis[0, cell_x, pl.ds(7 + cell_y, 1), :]
                stabilize = vis[1, cell_x, pl.ds(7 + cell_y, 1), :]
                total = total + viscosity * rows_at(x, y, 0, q) + stabilize * rows_at(x, y, 1, q)
            total = jnp.where(is_last, pltpu.roll(ends_row, LZ - 2 - y, 1), total)
            nod[pl.ds(y * 8, 8), :] = total
        for h in range(2):
            at = pl.multiple_of(x * LY + 8 * h, 8)
            flags = mk[pl.ds(at, 8), :]
            for c in range(4):
                near = nod[pl.ds(64 * h + c, 8, stride=8), :]
                far = nod[pl.ds(64 * h + 4 + c, 8, stride=8), :]
                value = near + pltpu.roll(far, 1, 1)
                if c == 2:
                    value = value - 2.0 * lat[pl.ds(at, 8), :]
                state = nat[pl.ds(pl.multiple_of(c * NODES + at, 8), 8), :]
                res[c, pl.ds(at, 8), :] = jnp.where((flags & (1 << c)) != 0, state, value)
        return carry

    puts = [put_t]
    for h in range(2):
        lax.fori_loop(h * LX // 2, (h + 1) * LX // 2, node_row, 0)
        part = pl.ds(h * NODES // 2, NODES // 2)
        puts.append(pltpu.make_async_copy(res.at[:, part], out_r.at[:, part], osem.at[1 + h]))
        puts[-1].start()
    for put in puts:
        put.wait()


def solution(mesh):
    sizes = nx, ny, nz = tuple(mesh.shape[a] for a in ("gx", "gy", "gz"))
    vmem = pltpu.VMEM
    hbm_spec = pl.BlockSpec(memory_space=pltpu.HBM)
    vmem_spec = pl.BlockSpec(memory_space=vmem)

    def in_hbm(a):
        return pltpu.with_memory_space_constraint(a, pltpu.HBM)

    def shards(heat, rate, guess, rock, mask, rheo, ops):
        kept = pl.pallas_call(
            functools.partial(exchange, sizes),
            out_shape=(
                vmem((8 * NODES, LZ), F32),
                vmem((NODES, LZ), jnp.int32),
                vmem((CX * CY, 96, LZ), F32),
                vmem((NODES, 8, LZ), F32),
                vmem((2, 96, PW), F32),
                vmem((2, CX, 24, LZ), F32),
                vmem((EX * TR, LZ), F32),
                vmem((2, 8, PW), F32),
                vmem((8, LZ), F32),
            ),
            in_specs=[hbm_spec] * 7,
            out_specs=[vmem_spec] * 9,
            scratch_shapes=[
                pltpu.SMEM((4,), F32),
                vmem((3, 32, 32), F32),
                vmem((3 * NODES, LZ), F32),
                vmem((NODES, LZ), jnp.int32),
                vmem((EX * TR, LZ), F32),
                vmem((EX * TR, LZ), F32),
                vmem((2, 8 * LY, LZ), F32),
                vmem((2, 8 * LY, LZ), F32),
                vmem((2, 8 * LX, LZ), F32),
                vmem((2, 8 * LX, LZ), F32),
                vmem((4, 8, LZ), F32),
                vmem((4, 8, LZ), F32),
                vmem((2, 8, LZ), F32),
                vmem((2, 8, LZ), F32),
                vmem((2, 8, PW), F32),
                vmem((2, 8, PW), F32),
                vmem((2, max(nx * ny, nz), 1, LZ), F32),
                vmem((EX * EY, 16, LZ), BF16),
                vmem((96, 128), BF16),
                pltpu.SemaphoreType.DMA((7,)),
                pltpu.SemaphoreType.DMA((20,)),
                pltpu.SemaphoreType.DMA((20,)),
                pltpu.SemaphoreType.DMA((2,)),
                pltpu.SemaphoreType.DMA((2,)),
            ],
            compiler_params=pltpu.CompilerParams(
                collective_id=0, has_side_effects=True, vmem_limit_bytes=24 * 1024 * 1024
            ),
        )(
            in_hbm(rheo),
            in_hbm(ops),
            in_hbm(heat.reshape(NODES, LZ)),
            in_hbm(rate.reshape(3 * NODES, LZ)),
            in_hbm(guess.reshape(4 * NODES, LZ)),
            in_hbm(rock.reshape(NODES, LZ)),
            in_hbm(mask.reshape(NODES, LZ)),
        )
        out_t, out_r = pl.pallas_call(
            finish,
            out_shape=(pltpu.HBM((NODES, LZ), F32), pltpu.HBM((4, NODES, LZ), F32)),
            in_specs=[vmem_spec] * 9,
            out_specs=[hbm_spec] * 2,
            scratch_shapes=[
                vmem((2, CX, 24, LZ), F32),
                vmem((8 * LY, LZ), F32),
                vmem((8, PW), F32),
                vmem((NODES, LZ), F32),
                vmem((4, NODES, LZ), F32),
                pltpu.SemaphoreType.DMA((3,)),
            ],
            compiler_params=pltpu.CompilerParams(vmem_limit_bytes=24 * 1024 * 1024),
        )(*(pltpu.with_memory_space_constraint(a, vmem) for a in kept))
        return out_t.reshape(LX, LY, LZ), out_r.reshape(4, LX, LY, LZ)

    grid = P("gx", "gy", "gz")
    fields = P(None, "gx", "gy", "gz")
    return jax.shard_map(
        shards,
        mesh=mesh,
        in_specs=(grid, fields, fields, grid, grid, P(), P()),
        out_specs=(grid, fields),
        check_vma=False,
    )
```
